512 devices in a mesh: feat: 64 (over z_hi, y, x), head: 8 (over z_lo, core).
Axes of the slice: x: 4, y: 8, z: 8 (z_hi: 2, z_lo: 4; z = z_hi * 4 + z_lo), core: 2. Of those that a mesh axis runs over, the one named last changes fastest.
Arguments:
- target_grads: bfloat16 [32, 5376], P('head', 'feat'), may hold values from -6 to 6
- positions: int32 [32], replicated, may hold values from 0 to 255
- raw_patterns: float32 [32, 32, 256], P('head'), may hold values from 0.02 to 1
- out_proj: bfloat16 [4096, 5376], P('head', 'feat'), may hold values from -0.078125 to 0.078125
- value_proj: bfloat16 [4096, 5376], P('head', 'feat'), may hold values from -0.5 to 0.5
- decoders: bfloat16 [24576, 5376], P('feat'), may hold values from -0.078125 to 0.078125
- feature_ids: int32 [256, 64], replicated, may hold values from 0 to 24575
- activations: float32 [256, 64], replicated, may hold values from 0.1 to 4
Outputs:
- edges: float32 [32, 256, 64], P('head')
The draws below stay inside these ranges and needn't reach their ends.
All inputs are finite; a program needn't handle non-finite values.
Results may differ from the reference program's by a relative error of at most 0.0044.
Values may be sent and summed in bfloat16 or wider, within the bound.
A program may use at most 128 MiB of HBM per device.

```python
import math
import jax
import jax.numpy as jnp
import numpy as np
from jax import lax

D = 5376
HEADS = 32
HD = 128
S = 256
K = 64
TARGETS = 32
FEATURES = 24576


def plant(values, stream_key, smallest, largest):
    shape = values.shape
    index_at = [jax.random.randint(jax.random.fold_in(stream_key, axis), (), 0, shape[axis]) for axis in range(len(shape))]
    values = values.at[tuple(index_at)].set(smallest)
    longest = shape.index(max(shape))
    index_at[longest] = (index_at[longest] + 1) % shape[longest]
    return values.at[tuple(index_at)].set(largest)


def block_scale(own_key, shape, cuts, least, top_value):
    loudness, own = 1.0, jax.random.fold_in(own_key, 6)
    for axis_at, blocks in cuts:
        steps = jnp.exp(jax.random.uniform(jax.random.fold_in(own, axis_at), (blocks,), jnp.float32, least / len(cuts), top_value / len(cuts)))
        loudness = loudness * jnp.repeat(steps, shape[axis_at] // blocks).reshape([-1 if axis == axis_at else 1 for axis in range(len(shape))])
    return loudness


def rank_table(count, lean):
    portions = [(1 << 20) // math.isqrt(grade ** lean) + 1 for grade in range(1, count + 1)]
    spread = 1 + sum(portions) // (1 << 30)
    return np.cumsum(np.array([max(1, weight // spread) for weight in portions]))


def ranked(rng, dims, count, skew):
    grid = rank_table(count, skew)
    lot = jax.random.randint(jax.random.fold_in(rng, 1), dims, 0, int(grid[count - 1]))
    standing = jnp.searchsorted(jnp.asarray(grid, jnp.int32), lot, side="right")
    return jax.random.permutation(jax.random.fold_in(rng, 2), count)[standing].astype(jnp.int32)


def normal_values(key, shape, deviation, reach, shards=(), held_as=jnp.bfloat16):
    result = jax.random.normal(key, shape, jnp.float32) * deviation
    if len(shards) > 0:
        result = block_scale(key, shape, shards, -0.22, 0.18) * result
    return jnp.clip(result, min=-reach, max=reach).astype(held_as)


def setup_inputs(seed: int = 0) -> dict:
    key_of = jax.random.split(jax.random.key(seed), 9)
    target_grads = normal_values(key_of[0], (TARGETS, D), 1.0, 6.0, ((0, 8), (1, 64)))
    positions = plant(jax.random.randint(key_of[1], (TARGETS,), 0, S), jax.random.fold_in(key_of[1], 1), 0, S - 1).astype(jnp.int32)
    raw_patterns = jnp.clip(jnp.exp(math.log(1.0) - 3.912023 * jax.random.uniform(key_of[2], (HEADS, TARGETS, S), jnp.float32) ** block_scale(key_of[2], (HEADS, TARGETS, S), ((0, 8),), -0.2, 0.2)), 0.02, 1.0)
    out_proj = normal_values(key_of[3], (HEADS * HD, D), D ** -0.5, 0.078125, ((0, 8), (1, 64)))
    value_proj = normal_values(key_of[4], (HEADS * HD, D), HD ** -0.5, 0.5, ((0, 8), (1, 64)))
    decoders = normal_values(key_of[5], (FEATURES, D), D ** -0.5, 0.078125, ((0, 64),))
    feature_ids = plant(ranked(key_of[6], (S, K), FEATURES, 2), jax.random.fold_in(key_of[6], 3), 0, FEATURES - 1).astype(jnp.int32)
    activations = jnp.clip(jnp.exp(jax.random.uniform(key_of[7], (S, K), jnp.float32, math.log(0.1), math.log(4.0))), 0.1, 4.0)
    return dict(target_grads=target_grads, positions=positions, raw_patterns=raw_patterns, out_proj=out_proj, value_proj=value_proj, decoders=decoders, feature_ids=feature_ids, activations=activations)


def reference(target_grads, positions, raw_patterns, out_proj, value_proj, decoders, feature_ids, activations):
    head_in = jnp.dot(target_grads, out_proj.T, preferred_element_type=jnp.float32).astype(jnp.bfloat16)
    head_in = head_in.reshape(TARGETS, HEADS, HD).astype(jnp.float32)
    values = value_proj.reshape(HEADS, HD, D).astype(jnp.float32)
    through = jnp.einsum("the,hed->thd", head_in, values, precision=lax.Precision.HIGHEST)
    spots = jnp.arange(S, dtype=jnp.int32)
    causal = (spots[None, :] <= positions[:, None]).astype(jnp.float32)
    masked = raw_patterns * causal[None, :, :]
    pattern = masked / jnp.sum(masked, axis=2, keepdims=True)
    attended = jnp.einsum("hts,thd->tsd", pattern, through, precision=lax.Precision.HIGHEST)
    direct = (spots[None, :] == positions[:, None]).astype(jnp.float32)
    panel = (attended + direct[:, :, None] * target_grads.astype(jnp.float32)[:, None, :]).astype(jnp.bfloat16)
    chosen = decoders[feature_ids].astype(jnp.float32)

    def score(row):
        return jnp.einsum("sd,skd->sk", row.astype(jnp.float32), chosen, precision=lax.Precision.HIGHEST)

    scores = lax.map(score, panel)
    return scores * activations[None, :, :]
```

```python
import functools

import jax
import jax.numpy as jnp
from jax import lax
from jax.experimental import pallas as pl
from jax.experimental.pallas import tpu as pltpu
from jax.sharding import PartitionSpec as P

MESH = pl.DeviceIdType.MESH
HD = 128
NZ, NY, NX, NH = 2, 8, 4, 8
NT = (((1,), (1,)), ((), ()))


def dot(a, b, dims=(((1,), (0,)), ((), ()))):
    return lax.dot_general(a, b, dims, preferred_element_type=jnp.float32)


def kernel(
    nz, ny, nx, nh, stop,
    pos_ref, grads_ref, raw_ref, outp_ref, valp_ref, dec_hbm, ids_ref, act_ref,
    out_ref,
    dec, gall, ga, gy, gfull, pall, psend, part, rs, ex, hall, tsend, tall, ablk, thr,
    eparts, ers, e1, eex, fin,
    dec_sem, ssem, rsem, ring_s, ring_r,
):
    f32, bf16 = jnp.float32, jnp.bfloat16
    na = nz * nx
    w = grads_ref.shape[1]
    wx = nx * w
    tokens = ids_ref.shape[0]
    feats = dec.shape[0]
    rows = nh * 16
    f = lax.axis_index("feat")
    g = lax.axis_index("head")
    x = lax.rem(f, nx)
    y = lax.rem(lax.div(f, nx), ny)
    z = lax.div(f, nx * ny)
    a = z * nx + x

    def head_at(d):
        j = lax.rem(g + d, nh)
        return j, (f, j)

    def y_at(d):
        j = lax.rem(y + d, ny)
        return j, (z * (nx * ny) + j * nx + x, g)

    def a_at(d):
        j = lax.rem(a + d, na)
        return j, (lax.div(j, nx) * (nx * ny) + y * nx + lax.rem(j, nx), g)

    groups = {"h": (head_at, nh), "y": (y_at, ny), "a": (a_at, na)}

    barrier = pltpu.get_barrier_semaphore()
    for at, n in groups.values():
        for d in range(1, n):
            pl.semaphore_signal(barrier, inc=1, device_id=at(d)[1], device_id_type=MESH)

    dec_copy = pltpu.make_async_copy(dec_hbm, dec, dec_sem)
    dec_copy.start()

    def exchange(stage, group, src, dst):
        at, n = groups[group]
        copies = []
        for d in range(1, n):
            j, device = at(d)
            copy = pltpu.make_async_remote_copy(
                src_ref=src(j),
                dst_ref=dst(d),
                send_sem=ssem.at[stage, d],
                recv_sem=rsem.at[stage, d],
                device_id=device,
                device_id_type=MESH,
            )
            copy.start()
            copies.append(copy)
        return copies

    def arrive(copies):
        for copy in copies:
            copy.wait_recv()

    pending = []

    own = grads_ref[...].astype(f32)
    mine = jnp.concatenate([own, own], axis=0)
    zero_lanes = jnp.zeros((8, gall.shape[2]), f32)
    gall[g] = zero_lanes
    gall[g, :, 0:w] = mine
    ga[a] = zero_lanes
    ga[a, :, 0:w] = mine
    pl.semaphore_wait(barrier, nh - 1 + ny - 1 + na - 1)
    c0 = exchange(0, "h", lambda j: gall.at[g], lambda d: gall.at[g])
    c2 = exchange(2, "a", lambda j: ga.at[a], lambda d: ga.at[a])

    for j in range(nh):
        for h in range(4):
            psend[j, 4 * h : 4 * h + 4, :] = raw_ref[h, 4 * j : 4 * j + 4, :]
    c1 = exchange(1, "h", lambda j: psend.at[j], lambda d: pall.at[g])
    pall[g] = psend[g]
    tsend[...] = jnp.zeros_like(tsend)

    arrive(c0)
    both = gall[...].reshape(nh * 8, gall.shape[2])[:, 0:w]
    low = lax.rem(lax.broadcasted_iota(jnp.int32, both.shape, 0), 8) < 4
    half = 2 * HD
    partial = dot(jnp.where(low, both, 0.0).astype(bf16), outp_ref[0:half, :], NT)
    partial += dot(jnp.where(low, 0.0, both).astype(bf16), outp_ref[half : 2 * half, :], NT)
    part[...] = partial.reshape(ny, 8, half)
    c4 = exchange(4, "y", lambda j: part.at[j], lambda d: rs.at[d])

    arrive(c2)
    for k in range(nz):
        for i in range(nx):
            gy[y, k, :, w * i : w * i + w] = ga[k * nx + i, :, 0:w]
    c3 = exchange(3, "y", lambda j: gy.at[y], lambda d: gy.at[y])

    arrive(c4)
    total = part[y]
    for d in range(1, ny):
        total += rs[d]
    ex[0] = total
    c5 = exchange(5, "a", lambda j: ex.at[0], lambda d: ex.at[d])
    arrive(c5)
    for d in range(1, na):
        total += ex[d]
    hall[y] = total.astype(bf16).astype(f32)
    c6 = exchange(6, "y", lambda j: hall.at[y], lambda d: hall.at[y])

    arrive(c1)
    raw = pall[...].reshape(rows, tokens)
    row_t = lax.rem(lax.broadcasted_iota(jnp.int32, raw.shape, 0), 4)
    spot = lax.broadcasted_iota(jnp.int32, raw.shape, 1)
    row_pos = jnp.zeros(raw.shape, jnp.int32)
    own_pos = []
    for t in range(4):
        own_pos.append(pos_ref[4 * g + t])
        row_pos = jnp.where(row_t == t, own_pos[t], row_pos)
    masked = jnp.where(spot <= row_pos, raw, 0.0)
    pattern = masked / jnp.sum(masked, axis=1, keepdims=True)
    pat = pattern.T
    pat_hi = pat.astype(bf16)
    pat_lo = (pat - pat_hi.astype(f32)).astype(bf16)

    arrive(c3)
    for k in range(nz):
        for j in range(ny):
            at = wx * (k * ny + j)
            gfull[:, at : at + wx] = gy[j, k, :, 0:wx]

    arrive(c6)
    hin = hall[...].reshape(ny * 8, half).astype(bf16)
    r = lax.broadcasted_iota(jnp.int32, (rows, ny * 8), 0)
    c = lax.broadcasted_iota(jnp.int32, (rows, ny * 8), 1)
    from_row = lax.div(r, 16) * 8 + lax.div(lax.rem(r, 16), 8) * 4 + lax.rem(r, 4)
    spread = dot((c == from_row).astype(bf16), hin)
    r = lax.broadcasted_iota(jnp.int32, (rows, half), 0)
    lane = lax.broadcasted_iota(jnp.int32, (rows, half), 1)
    fits = lax.rem(lax.div(r, 4), 2) == lax.div(lane, HD)
    upper = lax.rem(lax.div(r, 8), 2) == 1
    first = jnp.where(fits & ~upper, spread, 0.0).astype(bf16)
    second = jnp.where(fits & upper, spread, 0.0).astype(bf16)
    through = dot(first, valp_ref[0:half, :]) + dot(second, valp_ref[half : 2 * half, :])
    tsend[:, :, 0:w] = through.astype(bf16).reshape(nh, 16, w)
    c7 = exchange(7, "h", lambda j: tsend.at[j], lambda d: tall.at[g])
    tall[g] = tsend[g]

    dec_copy.wait()
    straight = dot(gfull[...].astype(bf16), dec[...], NT)

    arrive(c7)
    turned = tall[...].reshape(rows, tall.shape[2]).astype(f32).T
    ablk[a] = turned[0 : ablk.shape[1]].astype(bf16)
    c8 = exchange(8, "a", lambda j: ablk.at[a], lambda d: ablk.at[a])
    arrive(c8)
    for k in range(nz):
        joined = [ablk[k * nx + i].astype(f32)[0:w] for i in range(nx)]
        thr[k, y] = jnp.concatenate(joined, axis=0).astype(bf16)

    def hop(way, step, k):
        origin = lax.rem(y + (ny - step if way == 0 else step), ny)
        return pltpu.make_async_remote_copy(
            src_ref=thr.at[k, origin],
            dst_ref=thr.at[k, origin],
            send_sem=ring_s.at[way, step, k],
            recv_sem=ring_r.at[way, step, k],
            device_id=y_at(1 if way == 0 else ny - 1)[1],
            device_id_type=MESH,
        )

    def ring_has(way, step, k):
        if step < ny // 2 - 1:
            return True
        return step == ny // 2 - 1 and k == way

    hops = {}
    for step in range(ny // 2):
        for k in range(nz):
            for way in range(2):
                if not ring_has(way, step, k):
                    continue
                if step > 0:
                    hops[way, step - 1, k].wait_recv()
                hops[way, step, k] = hop(way, step, k)
                hops[way, step, k].start()
    for (way, step, k), copy in hops.items():
        if not ring_has(way, step + 1, k):
            copy.wait_recv()

    span = ny * wx
    scores = dot(dec[:, 0:span], thr[0].reshape(span, rows))
    for k in range(1, nz):
        scores += dot(dec[:, k * span : (k + 1) * span], thr[k].reshape(span, rows))
    sc_hi = scores.astype(bf16)
    sc_lo = (scores - sc_hi.astype(f32)).astype(bf16)
    right = jnp.concatenate([sc_hi, sc_hi, sc_lo], axis=1)

    ids = ids_ref[...] - f * feats
    ids = jnp.concatenate([ids, ids], axis=1)
    act = act_ref[...]
    act = jnp.concatenate([act, act], axis=1)
    lane = lax.broadcasted_iota(jnp.int32, ids.shape, 1)
    of_t = lax.rem(lax.broadcasted_iota(jnp.int32, pat.shape, 1), 4)
    token = lax.broadcasted_iota(jnp.int32, (tokens, feats), 0)
    piece = tokens // ny
    for p in range(2):
        picked = []
        for q in range(2):
            t = 2 * p + q
            hi = jnp.where(of_t == t, pat_hi, 0.0)
            lo = jnp.where(of_t == t, pat_lo, 0.0)
            left = jnp.concatenate([hi, lo, hi], axis=1)
            table = dot(left, right, NT)
            table += jnp.where(token == own_pos[t], straight[t : t + 1, :], 0.0)
            found = jnp.zeros(ids.shape, f32)
            for b in range(feats // 128):
                local = ids - 128 * b
                inside = (local >= 0) & (local < 128)
                taken = jnp.take_along_axis(
                    table[:, 128 * b : 128 * b + 128], jnp.clip(local, 0, 127), axis=1
                )
                found = jnp.where(inside, taken, found)
            picked.append(found)
        edge = jnp.where(lane < 64, picked[0], picked[1]) * act
        edge = edge.astype(bf16)
        for j in range(ny):
            eparts[j, p] = edge[piece * j : piece * (j + 1)]

    c10 = exchange(10, "y", lambda j: eparts.at[j], lambda d: ers.at[d])
    arrive(c10)
    total = eparts[y].astype(f32)
    for d in range(1, ny):
        total += ers[d].astype(f32)
    e1[...] = total.astype(bf16)
    c11 = exchange(11, "a", lambda j: e1, lambda d: eex.at[d])
    arrive(c11)
    for d in range(1, na):
        total += eex[d].astype(f32)
    fin[y] = total.astype(bf16)
    c12 = exchange(12, "y", lambda j: fin.at[y], lambda d: fin.at[y])
    arrive(c12)
    for j in range(ny):
        for p in range(2):
            block = fin[j, p].astype(f32)
            out_ref[2 * p, piece * j : piece * (j + 1), :] = block[:, 0:64]
            out_ref[2 * p + 1, piece * j : piece * (j + 1), :] = block[:, 64:128]

    for copies in (c0, c1, c2, c3, c4, c5, c6, c7, c8, c10, c11, c12):
        for copy in copies:
            copy.wait_send()
    for copy in hops.values():
        copy.wait_send()


def body(nz, ny, nx, nh, stop, grads, positions, raw, out_proj, value_proj, decoders, ids, act):
    f32, bf16 = jnp.float32, jnp.bfloat16
    w = grads.shape[1]
    tokens, listed = ids.shape
    feats, width = decoders.shape
    na, rows, piece = nz * nx, nh * 16, tokens // ny
    wx = nx * w
    lanes_w = -(-w // 128) * 128
    lanes_x = -(-wx // 128) * 128
    tall_w = -(-w // 16) * 16
    vmem = pltpu.VMEM
    scratch = [
        vmem((feats, width), bf16),
        vmem((nh, 8, lanes_w), f32),
        vmem((na, 8, lanes_w), f32),
        vmem((ny, nz, 8, lanes_x), f32),
        vmem((8, width), f32),
        vmem((nh, 16, tokens), f32),
        vmem((nh, 16, tokens), f32),
        vmem((ny, 8, 2 * HD), f32),
        vmem((ny, 8, 2 * HD), f32),
        vmem((na, 8, 2 * HD), f32),
        vmem((ny, 8, 2 * HD), f32),
        vmem((nh, 16, lanes_w), bf16),
        vmem((nh, 16, lanes_w), bf16),
        vmem((na, tall_w, rows), bf16),
        vmem((nz, ny, wx, rows), bf16),
        vmem((ny, 2, piece, 2 * listed), bf16),
        vmem((ny, 2, piece, 2 * listed), bf16),
        vmem((2, piece, 2 * listed), bf16),
        vmem((na, 2, piece, 2 * listed), bf16),
        vmem((ny, 2, piece, 2 * listed), bf16),
        pltpu.SemaphoreType.DMA,
        pltpu.SemaphoreType.DMA((13, 8)),
        pltpu.SemaphoreType.DMA((13, 8)),
        pltpu.SemaphoreType.DMA((2, max(ny // 2, 1), nz)),
        pltpu.SemaphoreType.DMA((2, max(ny // 2, 1), nz)),
    ]
    in_vmem = pl.BlockSpec(memory_space=pltpu.VMEM)
    return pl.pallas_call(
        functools.partial(kernel, nz, ny, nx, nh, stop),
        out_shape=jax.ShapeDtypeStruct((4, tokens, listed), f32),
        in_specs=[pl.BlockSpec(memory_space=pltpu.SMEM)]
        + [in_vmem] * 4
        + [pl.BlockSpec(memory_space=pl.ANY)]
        + [in_vmem] * 2,
        out_specs=in_vmem,
        scratch_shapes=scratch,
        compiler_params=pltpu.CompilerParams(
            collective_id=0, has_side_effects=True, vmem_limit_bytes=40 * 1024 * 1024
        ),
    )(positions, grads, raw, out_proj, value_proj, decoders, ids, act)


def solution(mesh, sizes=(NZ, NY, NX, NH), stop=99):
    placed = (
        P("head", "feat"),
        P(),
        P("head", None, None),
        P("head", "feat"),
        P("head", "feat"),
        P("feat", None),
        P(),
        P(),
    )
    return jax.shard_map(
        functools.partial(body, *sizes, stop),
        mesh=mesh,
        in_specs=placed,
        out_specs=P("head", None, None),
        check_vma=False,
    )
```

```python
import functools

import jax
import jax.numpy as jnp
from jax import lax
from jax.experimental import pallas as pl
from jax.experimental.pallas import tpu as pltpu
from jax.sharding import PartitionSpec as P

MESH = pl.DeviceIdType.MESH
HD = 128
NZ, NY, NX, NH = 2, 8, 4, 8
NT = (((1,), (1,)), ((), ()))


def dot(a, b, dims=(((1,), (0,)), ((), ()))):
    return lax.dot_general(a, b, dims, preferred_element_type=jnp.float32)


def kernel(
    nz, ny, nx, nh, stop,
    pos_ref, grads_ref, raw_hbm, outp_hbm, valp_hbm, dec_hbm, ids_hbm, act_hbm,
    out_ref,
    raw_ref, outp_ref, valp_ref, ids_ref, act_ref, dec, gall, ga, gy, gfull, pall, psend, part, rs, ex, hall, tsend, tall, ax, bx, thr,
    eparts, ers, e1, eex, fin, pats, ids_t,
    in_sem, ssem, rsem, side_s, side_r,
):
    f32, bf16 = jnp.float32, jnp.bfloat16
    na = nz * nx
    w = grads_ref.shape[1]
    wx = nx * w
    listed, tokens = ids_ref.shape
    feats = dec.shape[0]
    rows = nh * 16
    f = lax.axis_index("feat")
    g = lax.axis_index("head")
    x = lax.rem(f, nx)
    y = lax.rem(lax.div(f, nx), ny)
    z = lax.div(f, nx * ny)
    a = z * nx + x

    def head_at(d):
        j = lax.rem(g + d, nh)
        return j, (f, j)

    def y_at(d):
        j = lax.rem(y + d, ny)
        return j, (z * (nx * ny) + j * nx + x, g)

    def a_at(d):
        j = lax.rem(a + d, na)
        return j, (lax.div(j, nx) * (nx * ny) + y * nx + lax.rem(j, nx), g)

    def x_at(d):
        j = lax.rem(x + d, nx)
        return j, (f - x + j, g)

    def z_at(d):
        j = lax.rem(z + d, nz)
        return j, (f + (j - z) * (nx * ny), g)

    groups = {"h": (head_at, nh), "y": (y_at, ny), "a": (a_at, na), "x": (x_at, nx)}

    barrier = pltpu.get_barrier_semaphore()
    for name in ("h", "y", "a"):
        at, n = groups[name]
        for d in range(1, n):
            pl.semaphore_signal(barrier, inc=1, device_id=at(d)[1], device_id_type=MESH)

    loads = {}
    for i, (name, src, dst) in enumerate(
        (
            ("raw", raw_hbm, raw_ref),
            ("outp", outp_hbm, outp_ref),
            ("valp", valp_hbm, valp_ref.at[z]),
            ("ids", ids_hbm, ids_ref),
            ("act", act_hbm, act_ref),
            ("dec", dec_hbm, dec),
        )
    ):
        loads[name] = pltpu.make_async_copy(src, dst, in_sem.at[i])
        loads[name].start()

    def load(name):
        loads[name].wait()
        loaded.append(name)

    def exchange(stage, group, src, dst):
        at, n = groups[group]
        copies = []
        for d in range(1, n):
            j, device = at(d)
            copy = pltpu.make_async_remote_copy(
                src_ref=src(j),
                dst_ref=dst(d),
                send_sem=ssem.at[stage, d],
                recv_sem=rsem.at[stage, d],
                device_id=device,
                device_id_type=MESH,
            )
            copy.start()
            copies.append(copy)
            started.append(copy)
        return copies

    def send(slot, src, dst, device):
        copy = pltpu.make_async_remote_copy(
            src_ref=src,
            dst_ref=dst,
            send_sem=side_s.at[slot],
            recv_sem=side_r.at[slot],
            device_id=device,
            device_id_type=MESH,
        )
        copy.start()
        started.append(copy)
        return copy

    def arrive(copies):
        for copy in copies:
            copy.wait_recv()
            arrived.append(copy)

    def finish():
        for copy in started:
            if not any(copy is other for other in arrived):
                copy.wait_recv()
            copy.wait_send()
        for name, copy in loads.items():
            if name not in loaded:
                copy.wait()

    started, arrived, loaded = [], [], []

    own = grads_ref[...].astype(f32)
    mine = jnp.concatenate([own, own], axis=0)
    zero_lanes = jnp.zeros((8, gall.shape[2]), f32)
    gall[g] = zero_lanes
    gall[g, :, 0:w] = mine
    ga[a] = zero_lanes
    ga[a, :, 0:w] = mine
    pl.semaphore_wait(barrier, nh - 1 + ny - 1 + na - 1)
    c0 = exchange(0, "h", lambda j: gall.at[g], lambda d: gall.at[g])
    load("valp")
    cv = send(0, valp_ref.at[z], valp_ref.at[z], z_at(1)[1])

    load("raw")
    for j in range(nh):
        for h in range(4):
            psend[j, 4 * h : 4 * h + 4, :] = raw_ref[h, 4 * j : 4 * j + 4, :]
    tsend[...] = jnp.zeros_like(tsend)
    load("outp")

    arrive(c0)
    if stop <= 0:
        return finish()
    both = gall[...].reshape(nh * 8, gall.shape[2])[:, 0:w]
    low = lax.rem(lax.broadcasted_iota(jnp.int32, both.shape, 0), 8) < 4
    half = 2 * HD
    partial = dot(jnp.where(low, both, 0.0).astype(bf16), outp_ref[:, 0:half])
    partial += dot(jnp.where(low, 0.0, both).astype(bf16), outp_ref[:, half : 2 * half])
    part[...] = partial.reshape(ny, 8, half)
    c4 = exchange(4, "y", lambda j: part.at[j], lambda d: rs.at[d])
    c1 = exchange(1, "h", lambda j: psend.at[j], lambda d: pall.at[g])
    pall[g] = psend[g]
    c2 = exchange(2, "a", lambda j: ga.at[a], lambda d: ga.at[a])

    arrive(c4)
    if stop <= 4:
        return finish()
    total = part[y]
    for d in range(1, ny):
        total += rs[d]
    ex[0] = total
    c5 = exchange(5, "a", lambda j: ex.at[0], lambda d: ex.at[d])

    arrive(c2)
    for k in range(nz):
        for i in range(nx):
            gy[y, k, :, w * i : w * i + w] = ga[k * nx + i, :, 0:w]

    r = lax.broadcasted_iota(jnp.int32, (rows, ny * 8), 0)
    c = lax.broadcasted_iota(jnp.int32, (rows, ny * 8), 1)
    from_row = lax.div(r, 16) * 8 + lax.div(lax.rem(r, 16), 8) * 4 + lax.rem(r, 4)
    choose = (c == from_row).astype(bf16)
    r = lax.broadcasted_iota(jnp.int32, (rows, half), 0)
    lane = lax.broadcasted_iota(jnp.int32, (rows, half), 1)
    fits = lax.rem(lax.div(r, 4), 2) == lax.div(lane, HD)
    upper = lax.rem(lax.div(r, 8), 2) == 1

    arrive(c5)
    if stop <= 5:
        return finish()
    for d in range(1, na):
        total += ex[d]
    hall[y] = total.astype(bf16).astype(f32)
    c6 = exchange(6, "y", lambda j: hall.at[y], lambda d: hall.at[y])

    arrive(c1)
    raw = pall[...].reshape(rows, tokens)
    row_t = lax.rem(lax.broadcasted_iota(jnp.int32, raw.shape, 0), 4)
    spot = lax.broadcasted_iota(jnp.int32, raw.shape, 1)
    row_pos = jnp.zeros(raw.shape, jnp.int32)
    own_pos = []
    for t in range(4):
        own_pos.append(pos_ref[4 * g + t])
        row_pos = jnp.where(row_t == t, own_pos[t], row_pos)
    masked = jnp.where(spot <= row_pos, raw, 0.0)
    pattern = masked / jnp.sum(masked, axis=1, keepdims=True)
    pat = pattern.T
    pat_hi = pat.astype(bf16)
    pat_lo = (pat - pat_hi.astype(f32)).astype(bf16)
    pats[0] = pat_hi
    pats[1] = pat_lo

    arrive([cv])
    arrive(c6)
    if stop <= 6:
        return finish()
    hin = hall[...].reshape(ny * 8, half).astype(bf16)
    spread = dot(choose, hin)
    first = jnp.where(fits & ~upper, spread, 0.0).astype(bf16)
    second = jnp.where(fits & upper, spread, 0.0).astype(bf16)
    for k in range(nz):
        through = dot(first, valp_ref[k, :, 0:half], NT)
        through += dot(second, valp_ref[k, :, half : 2 * half], NT)
        tsend[:, k, :, 0:w] = through.astype(bf16).reshape(nh, 16, w)
    c7 = exchange(7, "h", lambda j: tsend.at[j], lambda d: tall.at[g])
    tall[g] = tsend[g]
    c3 = exchange(3, "y", lambda j: gy.at[y], lambda d: gy.at[y])

    load("ids")
    load("act")
    ids = ids_ref[...] - f * feats
    ids_t[...] = jnp.concatenate([ids, ids], axis=0).T

    arrive(c7)
    if stop <= 7:
        return finish()
    tall_w = ax.shape[1]

    def turned(k):
        block = tall[:, k].reshape(rows, tall.shape[3]).astype(f32).T
        return block[0:tall_w].astype(bf16)

    ax[x] = turned(0)
    cx = exchange(8, "x", lambda j: ax.at[x], lambda d: ax.at[x])
    bx[x, 0] = turned(1)
    cy = exchange(9, "y", lambda j: bx.at[x, 0], lambda d: bx.at[x, d])
    right, left = x_at(1)[1], x_at(nx - 1)[1]
    from_left, from_right = x_at(nx - 1)[0], x_at(1)[0]
    hops = {}

    def pass_on(d):
        hops["r", d] = send(20 + 2 * d, bx.at[x, d], bx.at[x, d], right)
        hops["l", d] = send(21 + 2 * d, bx.at[x, d], bx.at[x, d], left)

    pass_on(0)
    arrive(cx)
    joined = [ax[i].astype(f32)[0:w] for i in range(nx)]
    thr[0, y] = jnp.concatenate(joined, axis=0).astype(bf16)
    mine_y = thr.at[0, y]
    far = {}
    steps = (2, ny - 2, 1, ny - 1) if ny == 8 else (1,)
    for i, d in enumerate(steps):
        far[d] = send(1 + i, mine_y, mine_y, y_at(d)[1])
    order = (1, ny - 1, 2, ny - 2, 3, ny - 3, 4) if ny == 8 else (1,)
    for d in order:
        arrive([cy[d - 1]])
        pass_on(d)

    load("dec")
    arrive(c3)
    for k in range(nz):
        for j in range(ny):
            at = wx * (k * ny + j)
            gfull[:, at : at + wx] = gy[j, k, :, 0:wx]

    cut = (wx // 32) * 16
    if ny == 8:
        arrive([far[2]])
        back = thr.at[0, y_at(ny - 2)[0]]
        far[3] = send(5, back, back, y_at(1)[1])
        back = thr.at[0, y_at(ny - 2)[0], 0:cut]
        far["low"] = send(6, back, back, y_at(2)[1])
        arrive([far[ny - 2]])
        back = thr.at[0, y_at(2)[0]]
        far[ny - 3] = send(7, back, back, y_at(ny - 1)[1])
        back = thr.at[0, y_at(2)[0], cut:wx]
        far["high"] = send(8, back, back, y_at(ny - 2)[1])
    for d in (0,) + order:
        arrive([hops["r", d]])
        if d <= ny // 2 - 1:
            hops["r2", d] = send(40 + d, bx.at[from_left, d], bx.at[from_left, d], right)
        arrive([hops["l", d]])
        if d > ny // 2 - 1:
            hops["l2", d] = send(40 + d, bx.at[from_right, d], bx.at[from_right, d], left)

    straight = dot(gfull[...].astype(bf16), dec[...], NT)

    for d in far:
        if not any(far[d] is other for other in arrived):
            arrive([far[d]])
    span = ny * wx
    scores = dot(dec[:, 0:span], thr[0].reshape(span, rows))
    for d in range(ny):
        arrive([hops["r2" if d <= ny // 2 - 1 else "l2", d]])
    if stop <= 9:
        return finish()
    for d in range(ny):
        joined = [bx[i, d].astype(f32)[0:w] for i in range(nx)]
        thr[1, y_at(ny - d)[0]] = jnp.concatenate(joined, axis=0).astype(bf16)
    scores += dot(dec[:, span : 2 * span], thr[1].reshape(span, rows))
    sc_hi = scores.astype(bf16)
    sc_lo = (scores - sc_hi.astype(f32)).astype(bf16)
    right = jnp.concatenate([sc_hi, sc_hi, sc_lo], axis=1)

    ids = ids_t[...]
    act = act_ref[...]
    act = jnp.concatenate([act, act], axis=0)
    lane = lax.broadcasted_iota(jnp.int32, ids.shape, 1)
    pat_hi, pat_lo = pats[0], pats[1]
    of_t = lax.rem(lax.broadcasted_iota(jnp.int32, pat_hi.shape, 1), 4)
    token = lax.broadcasted_iota(jnp.int32, (tokens, feats), 0)
    piece = 2 * listed // ny
    for p in range(2):
        picked = []
        for q in range(2):
            t = 2 * p + q
            hi = jnp.where(of_t == t, pat_hi, 0.0)
            lo = jnp.where(of_t == t, pat_lo, 0.0)
            left = jnp.concatenate([hi, lo, hi], axis=1)
            table = dot(left, right, NT)
            table += jnp.where(token == own_pos[t], straight[t : t + 1, :], 0.0)
            found = jnp.zeros(ids.shape, f32)
            for b in range(feats // 128):
                local = ids - 128 * b
                inside = (local >= 0) & (local < 128)
                taken = jnp.take_along_axis(
                    table[:, 128 * b : 128 * b + 128], jnp.clip(local, 0, 127), axis=1
                )
                found = jnp.where(inside, taken, found)
            picked.append(found)
        edge = jnp.where(lane < listed, picked[0], picked[1]).T * act
        edge = edge.astype(bf16)
        for j in range(ny):
            eparts[j, p] = edge[piece * j : piece * (j + 1)]

    c10 = exchange(10, "y", lambda j: eparts.at[j], lambda d: ers.at[d])
    arrive(c10)
    if stop <= 10:
        return finish()
    total = eparts[y].astype(f32)
    for d in range(1, ny):
        total += ers[d].astype(f32)
    e1[...] = total.astype(bf16)
    c11 = exchange(11, "a", lambda j: e1, lambda d: eex.at[d])
    arrive(c11)
    if stop <= 11:
        return finish()
    for d in range(1, na):
        total += eex[d].astype(f32)
    fin[y] = total.astype(bf16)
    c12 = exchange(12, "y", lambda j: fin.at[y], lambda d: fin.at[y])
    arrive(c12)
    if stop <= 12:
        return finish()
    for j in range(ny):
        for p in range(2):
            out_ref[p, piece * j : piece * (j + 1), :] = fin[j, p].astype(f32)

    finish()


def body(nz, ny, nx, nh, stop, cid, grads, positions, raw, out_proj, value_proj, decoders, ids, act):
    f32, bf16 = jnp.float32, jnp.bfloat16
    out_proj, value_proj, ids, act = out_proj.T, value_proj.T, ids.T, act.T
    w = grads.shape[1]
    listed, tokens = ids.shape
    feats, width = decoders.shape
    na, rows, piece = nz * nx, nh * 16, 2 * listed // ny
    wx = nx * w
    lanes_w = -(-w // 128) * 128
    lanes_x = -(-wx // 128) * 128
    tall_w = -(-w // 16) * 16
    vmem = pltpu.VMEM
    scratch = [
        vmem(raw.shape, f32),
        vmem(out_proj.shape, bf16),
        vmem((nz,) + value_proj.shape, bf16),
        vmem(ids.shape, jnp.int32),
        vmem(act.shape, f32),
        vmem((feats, width), bf16),
        vmem((nh, 8, lanes_w), f32),
        vmem((na, 8, lanes_w), f32),
        vmem((ny, nz, 8, lanes_x), f32),
        vmem((8, width), f32),
        vmem((nh, 16, tokens), f32),
        vmem((nh, 16, tokens), f32),
        vmem((ny, 8, 2 * HD), f32),
        vmem((ny, 8, 2 * HD), f32),
        vmem((na, 8, 2 * HD), f32),
        vmem((ny, 8, 2 * HD), f32),
        vmem((nh, nz, 16, lanes_w), bf16),
        vmem((nh, nz, 16, lanes_w), bf16),
        vmem((nx, tall_w, rows), bf16),
        vmem((nx, ny, tall_w, rows), bf16),
        vmem((nz, ny, wx, rows), bf16),
        vmem((ny, 2, piece, tokens), bf16),
        vmem((ny, 2, piece, tokens), bf16),
        vmem((2, piece, tokens), bf16),
        vmem((na, 2, piece, tokens), bf16),
        vmem((ny, 2, piece, tokens), bf16),
        vmem((2, tokens, rows), bf16),
        vmem((tokens, 2 * listed), jnp.int32),
        pltpu.SemaphoreType.DMA((6,)),
        pltpu.SemaphoreType.DMA((13, 8)),
        pltpu.SemaphoreType.DMA((13, 8)),
        pltpu.SemaphoreType.DMA((48,)),
        pltpu.SemaphoreType.DMA((48,)),
    ]
    in_vmem = pl.BlockSpec(memory_space=pltpu.VMEM)
    edges = pl.pallas_call(
        functools.partial(kernel, nz, ny, nx, nh, stop),
        out_shape=jax.ShapeDtypeStruct((2, 2 * listed, tokens), f32),
        in_specs=[pl.BlockSpec(memory_space=pltpu.SMEM), in_vmem]
        + [pl.BlockSpec(memory_space=pl.ANY)] * 6,
        out_specs=in_vmem,
        scratch_shapes=scratch,
        compiler_params=pltpu.CompilerParams(
            collective_id=cid, has_side_effects=True, vmem_limit_bytes=60 * 1024 * 1024
        ),
    )(positions, grads, raw, out_proj, value_proj, decoders, ids, act)
    return edges.reshape(4, listed, tokens).transpose(0, 2, 1)


def solution(mesh, sizes=(NZ, NY, NX, NH), stop=99, cid=0):
    placed = (
        P("head", "feat"),
        P(),
        P("head", None, None),
        P("head", "feat"),
        P("head", "feat"),
        P("feat", None),
        P(),
        P(),
    )
    return jax.shard_map(
        functools.partial(body, *sizes, stop, cid),
        mesh=mesh,
        in_specs=placed,
        out_specs=P("head", None, None),
        check_vma=False,
    )
```

```python
import functools

import jax
import jax.numpy as jnp
from jax import lax
from jax.experimental import pallas as pl
from jax.experimental.pallas import tpu as pltpu
from jax.sharding import PartitionSpec as P

MESH = pl.DeviceIdType.MESH
HD = 128
NZ, NY, NX, NH = 2, 8, 4, 8
NT = (((1,), (1,)), ((), ()))


def dot(a, b, dims=(((1,), (0,)), ((), ()))):
    return lax.dot_general(a, b, dims, preferred_element_type=jnp.float32)


def kernel(
    nz, ny, nx, nh, stop,
    pos_ref, grads_ref, raw_hbm, outp_hbm, valp_hbm, dec_hbm, ids_hbm, act_hbm,
    out_ref,
    raw_ref, outp_ref, valp_ref, ids_ref, act_ref, dec, gall, ga, gy, gfull, pall, psend, part, rs, ex, hall, tsend, tall, ax, bx, thr,
    eparts, ers, e1, eex, fin, pats, ids_t,
    in_sem, ssem, rsem, side_s, side_r,
):
    f32, bf16 = jnp.float32, jnp.bfloat16
    na = nz * nx
    w = grads_ref.shape[1]
    wx = nx * w
    listed, tokens = ids_ref.shape
    feats = dec.shape[0]
    rows = nh * 16
    f = lax.axis_index("feat")
    g = lax.axis_index("head")
    x = lax.rem(f, nx)
    y = lax.rem(lax.div(f, nx), ny)
    z = lax.div(f, nx * ny)
    a = z * nx + x

    def place(dz, dy, dx, dh):
        zj, yj, xj = lax.rem(z + dz, nz), lax.rem(y + dy, ny), lax.rem(x + dx, nx)
        gj = lax.rem(g + dh, nh)
        return zj, yj, xj, gj, (zj * (nx * ny) + yj * nx + xj, gj)

    def far_first(n):
        return sorted(range(1, n), key=lambda d: -min(d, n - d))

    groups = {
        "h": [(d, place(0, 0, 0, d)) for d in far_first(nh)],
        "y": [(d, place(0, d, 0, 0)) for d in far_first(ny)],
        "x": [(d, place(0, 0, d, 0)) for d in far_first(nx)],
        "a": [(nx * k + d, place(k, 0, d, 0)) for k in range(1, nz) for d in far_first(nx) + [0]]
        + [(d, place(0, 0, d, 0)) for d in far_first(nx)],
        "zh": [(nh * k + d, place(k, 0, 0, d)) for k in range(1, nz) for d in [0, 1, nh - 1]]
        + [(d, place(0, 0, 0, d)) for d in far_first(nh)]
        + [(nh * k + d, place(k, 0, 0, d)) for k in range(1, nz) for d in range(2, nh - 1)],
    }
    if nh == 2:
        groups["zh"] = [(2, place(1, 0, 0, 0)), (3, place(1, 0, 0, 1)), (1, place(0, 0, 0, 1))]

    barrier = pltpu.get_barrier_semaphore()
    greet = groups["a"] + groups["y"] + groups["zh"]
    greet = [who for slot, who in greet if not (who is groups["zh"][0][1])]
    for who in greet:
        pl.semaphore_signal(barrier, inc=1, device_id=who[4], device_id_type=MESH)

    loads = {}
    for i, (name, src, dst) in enumerate(
        (
            ("raw", raw_hbm, raw_ref),
            ("outp", outp_hbm, outp_ref),
            ("valp", valp_hbm, valp_ref),
            ("ids", ids_hbm, ids_ref),
            ("act", act_hbm, act_ref),
            ("dec", dec_hbm, dec),
        )
    ):
        loads[name] = pltpu.make_async_copy(src, dst, in_sem.at[i])
        loads[name].start()

    def load(name):
        loads[name].wait()
        loaded.append(name)

    def exchange(stage, group, src, dst):
        copies = {}
        for slot, who in groups[group]:
            copies[slot] = pltpu.make_async_remote_copy(
                src_ref=src(who),
                dst_ref=dst(slot),
                send_sem=ssem.at[stage, slot],
                recv_sem=rsem.at[stage, slot],
                device_id=who[4],
                device_id_type=MESH,
            )
            copies[slot].start()
            started.append(copies[slot])
        return copies

    def send(slot, src, dst, device):
        copy = pltpu.make_async_remote_copy(
            src_ref=src,
            dst_ref=dst,
            send_sem=side_s.at[slot],
            recv_sem=side_r.at[slot],
            device_id=device,
            device_id_type=MESH,
        )
        copy.start()
        started.append(copy)
        return copy

    def arrive(copies):
        for copy in copies.values() if isinstance(copies, dict) else copies:
            copy.wait_recv()
            arrived.append(copy)

    def finish():
        for copy in started:
            if not any(copy is other for other in arrived):
                copy.wait_recv()
            copy.wait_send()
        for name, copy in loads.items():
            if name not in loaded:
                copy.wait()

    started, arrived, loaded = [], [], []

    own = grads_ref[...].astype(f32)
    mine = jnp.concatenate([own, own], axis=0)
    zero_lanes = jnp.zeros((8, gall.shape[2]), f32)
    gall[g] = zero_lanes
    gall[g, :, 0:w] = mine
    ga[a] = zero_lanes
    ga[a, :, 0:w] = mine
    pl.semaphore_wait(barrier, len(greet))
    c0 = exchange(0, "h", lambda j: gall.at[g], lambda d: gall.at[g])

    load("raw")
    for j in range(nh):
        for h in range(4):
            psend[j, 4 * h : 4 * h + 4, :] = raw_ref[h, 4 * j : 4 * j + 4, :]
    tsend[...] = jnp.zeros_like(tsend)
    gfull[...] = jnp.zeros_like(gfull)
    load("outp")

    arrive(c0)
    if stop <= 0:
        return finish()
    both = gall[...].reshape(nh * 8, gall.shape[2])[:, 0:w]
    low = lax.rem(lax.broadcasted_iota(jnp.int32, both.shape, 0), 8) < 4
    half = 2 * HD
    partial = dot(jnp.where(low, both, 0.0).astype(bf16), outp_ref[:, 0:half])
    partial += dot(jnp.where(low, 0.0, both).astype(bf16), outp_ref[:, half : 2 * half])
    part[...] = partial.reshape(ny, 8, half)
    c4 = exchange(4, "y", lambda who: part.at[who[1]], lambda d: rs.at[d])
    c2 = exchange(2, "a", lambda j: ga.at[a], lambda d: ga.at[a])

    arrive(c4)
    if stop <= 4:
        return finish()
    total = part[y]
    for d in range(1, ny):
        total += rs[d]
    ex[0] = total
    c5 = exchange(5, "a", lambda j: ex.at[0], lambda d: ex.at[d])

    arrive(c2)
    for k in range(nz):
        for i in range(nx):
            gy[y, 4 * k : 4 * k + 4, w * i : w * i + w] = ga[k * nx + i, 0:4, 0:w]
    c3 = exchange(3, "y", lambda j: gy.at[y], lambda d: gy.at[y])

    r = lax.broadcasted_iota(jnp.int32, (rows, ny * 8), 0)
    c = lax.broadcasted_iota(jnp.int32, (rows, ny * 8), 1)
    from_row = lax.div(r, 16) * 8 + lax.div(lax.rem(r, 16), 8) * 4 + lax.rem(r, 4)
    choose = (c == from_row).astype(bf16)
    r = lax.broadcasted_iota(jnp.int32, (rows, half), 0)
    lane = lax.broadcasted_iota(jnp.int32, (rows, half), 1)
    fits = lax.rem(lax.div(r, 4), 2) == lax.div(lane, HD)
    upper = lax.rem(lax.div(r, 8), 2) == 1

    arrive(c5)
    if stop <= 5:
        return finish()
    for d in range(1, na):
        total += ex[d]
    hall[y] = total.astype(bf16).astype(f32)
    c6 = exchange(6, "y", lambda j: hall.at[y], lambda d: hall.at[y])

    arrive(c6)
    if stop <= 6:
        return finish()
    hin = hall[...].reshape(ny * 8, half).astype(bf16)
    spread = dot(choose, hin)
    first = jnp.where(fits & ~upper, spread, 0.0).astype(bf16)
    second = jnp.where(fits & upper, spread, 0.0).astype(bf16)
    load("valp")
    through = dot(first, valp_ref[:, 0:half], NT)
    through += dot(second, valp_ref[:, half : 2 * half], NT)
    tsend[:, :, 0:w] = through.astype(bf16).reshape(nh, 16, w)
    c7 = exchange(7, "zh", lambda who: tsend.at[who[3]], lambda d: tall.at[z, g])
    tall[z, g] = tsend[g]

    load("ids")
    load("act")
    ids = ids_ref[...] - f * feats
    ids_t[...] = jnp.concatenate([ids, ids], axis=0).T

    arrive(c7)
    if stop <= 7:
        return finish()
    tall_w = ax.shape[1]

    def turned(k):
        block = tall[k].reshape(rows, tall.shape[3]).astype(f32).T
        return block[0:tall_w].astype(bf16)

    ax[x] = turned(0)
    cx = exchange(8, "x", lambda j: ax.at[x], lambda d: ax.at[x])
    bx[x, 0] = turned(1)
    cy = exchange(9, "y", lambda j: bx.at[x, 0], lambda d: bx.at[x, d])
    right, left = place(0, 0, 1, 0)[4], place(0, 0, nx - 1, 0)[4]
    from_left, from_right = lax.rem(x + nx - 1, nx), lax.rem(x + 1, nx)

    def y_at(d):
        who = place(0, d, 0, 0)
        return who[1], who[4]

    hops = {}

    def pass_on(d):
        hops["r", d] = send(20 + 2 * d, bx.at[x, d], bx.at[x, d], right)
        hops["l", d] = send(21 + 2 * d, bx.at[x, d], bx.at[x, d], left)

    pass_on(0)
    arrive(cx)
    joined = [ax[i].astype(f32)[0:w] for i in range(nx)]
    thr[0, y] = jnp.concatenate(joined, axis=0).astype(bf16)
    mine_y = thr.at[0, y]
    far = {}
    steps = (2, ny - 2, 1, ny - 1) if ny == 8 else (1,)
    for i, d in enumerate(steps):
        far[d] = send(1 + i, mine_y, mine_y, y_at(d)[1])
    order = (1, ny - 1, 2, ny - 2, 3, ny - 3, 4) if ny == 8 else (1,)
    for d in order:
        arrive([cy[d]])
        pass_on(d)
    c1 = exchange(1, "h", lambda who: psend.at[who[3]], lambda d: pall.at[g])
    pall[g] = psend[g]

    load("dec")
    arrive(c3)
    for k in range(nz):
        for j in range(ny):
            at = wx * (k * ny + j)
            gfull[0:4, at : at + wx] = gy[j, 4 * k : 4 * k + 4, 0:wx]

    cut = (wx // 32) * 16
    if ny == 8:
        arrive([far[2]])
        back = thr.at[0, y_at(ny - 2)[0]]
        far[3] = send(5, back, back, y_at(1)[1])
        back = thr.at[0, y_at(ny - 2)[0], 0:cut]
        far["low"] = send(6, back, back, y_at(2)[1])
        arrive([far[ny - 2]])
        back = thr.at[0, y_at(2)[0]]
        far[ny - 3] = send(7, back, back, y_at(ny - 1)[1])
        back = thr.at[0, y_at(2)[0], cut:wx]
        far["high"] = send(8, back, back, y_at(ny - 2)[1])
    for d in (0,) + order:
        arrive([hops["r", d]])
        if d <= ny // 2 - 1:
            hops["r2", d] = send(40 + d, bx.at[from_left, d], bx.at[from_left, d], right)
        arrive([hops["l", d]])
        if d > ny // 2 - 1:
            hops["l2", d] = send(40 + d, bx.at[from_right, d], bx.at[from_right, d], left)

    arrive(c1)
    raw = pall[...].reshape(rows, tokens)
    row_t = lax.rem(lax.broadcasted_iota(jnp.int32, raw.shape, 0), 4)
    spot = lax.broadcasted_iota(jnp.int32, raw.shape, 1)
    row_pos = jnp.zeros(raw.shape, jnp.int32)
    own_pos = []
    for t in range(4):
        own_pos.append(pos_ref[4 * g + t])
        row_pos = jnp.where(row_t == t, own_pos[t], row_pos)
    masked = jnp.where(spot <= row_pos, raw, 0.0)
    pattern = masked / jnp.sum(masked, axis=1, keepdims=True)
    pat = pattern.T
    pat_hi = pat.astype(bf16)
    pat_lo = (pat - pat_hi.astype(f32)).astype(bf16)
    pats[0] = pat_hi
    pats[1] = pat_lo

    straight = dot(gfull[...].astype(bf16), dec[...], NT)

    for d in far:
        if not any(far[d] is other for other in arrived):
            arrive([far[d]])
    span = ny * wx
    scores = dot(dec[:, 0:span], thr[0].reshape(span, rows))
    for d in range(ny):
        arrive([hops["r2" if d <= ny // 2 - 1 else "l2", d]])
    if stop <= 9:
        return finish()
    for d in range(ny):
        joined = [bx[i, d].astype(f32)[0:w] for i in range(nx)]
        thr[1, y_at(ny - d)[0]] = jnp.concatenate(joined, axis=0).astype(bf16)
    scores += dot(dec[:, span : 2 * span], thr[1].reshape(span, rows))
    sc_hi = scores.astype(bf16)
    sc_lo = (scores - sc_hi.astype(f32)).astype(bf16)
    right = jnp.concatenate([sc_hi, sc_hi, sc_lo], axis=1)

    ids = ids_t[...]
    act = act_ref[...]
    act = jnp.concatenate([act, act], axis=0)
    lane = lax.broadcasted_iota(jnp.int32, ids.shape, 1)
    pat_hi, pat_lo = pats[0], pats[1]
    of_t = lax.rem(lax.broadcasted_iota(jnp.int32, pat_hi.shape, 1), 4)
    token = lax.broadcasted_iota(jnp.int32, (tokens, feats), 0)
    piece = 2 * listed // ny
    for p in range(2):
        picked = []
        for q in range(2):
            t = 2 * p + q
            hi = jnp.where(of_t == t, pat_hi, 0.0)
            lo = jnp.where(of_t == t, pat_lo, 0.0)
            left = jnp.concatenate([hi, lo, hi], axis=1)
            table = dot(left, right, NT)
            table += jnp.where(token == own_pos[t], straight[t : t + 1, :], 0.0)
            found = jnp.zeros(ids.shape, f32)
            for b in range(feats // 128):
                local = ids - 128 * b
                inside = (local >= 0) & (local < 128)
                taken = jnp.take_along_axis(
                    table[:, 128 * b : 128 * b + 128], jnp.clip(local, 0, 127), axis=1
                )
                found = jnp.where(inside, taken, found)
            picked.append(found)
        edge = jnp.where(lane < listed, picked[0], picked[1]).T * act
        edge = edge.astype(bf16)
        for j in range(ny):
            eparts[j, p] = edge[piece * j : piece * (j + 1)]

    c10 = exchange(10, "y", lambda who: eparts.at[who[1]], lambda d: ers.at[d])
    arrive(c10)
    if stop <= 10:
        return finish()
    total = eparts[y].astype(f32)
    for d in range(1, ny):
        total += ers[d].astype(f32)
    e1[...] = total.astype(bf16)
    c11 = exchange(11, "a", lambda j: e1, lambda d: eex.at[d])
    arrive(c11)
    if stop <= 11:
        return finish()
    for d in range(1, na):
        total += eex[d].astype(f32)
    fin[y] = total.astype(bf16)
    c12 = exchange(12, "y", lambda j: fin.at[y], lambda d: fin.at[y])
    arrive(c12)
    if stop <= 12:
        return finish()
    for j in range(ny):
        for p in range(2):
            out_ref[p, piece * j : piece * (j + 1), :] = fin[j, p]

    finish()


def body(nz, ny, nx, nh, stop, cid, grads, positions, raw, out_proj, value_proj, decoders, ids, act):
    f32, bf16 = jnp.float32, jnp.bfloat16
    out_proj, value_proj, ids, act = out_proj.T, value_proj.T, ids.T, act.T
    w = grads.shape[1]
    listed, tokens = ids.shape
    feats, width = decoders.shape
    na, rows, piece = nz * nx, nh * 16, 2 * listed // ny
    wx = nx * w
    lanes_w = -(-w // 128) * 128
    lanes_x = -(-wx // 128) * 128
    tall_w = -(-w // 16) * 16
    vmem = pltpu.VMEM
    scratch = [
        vmem(raw.shape, f32),
        vmem(out_proj.shape, bf16),
        vmem(value_proj.shape, bf16),
        vmem(ids.shape, jnp.int32),
        vmem(act.shape, f32),
        vmem((feats, width), bf16),
        vmem((nh, 8, lanes_w), f32),
        vmem((na, 8, lanes_w), f32),
        vmem((ny, 8, lanes_x), f32),
        vmem((8, width), f32),
        vmem((nh, 16, tokens), f32),
        vmem((nh, 16, tokens), f32),
        vmem((ny, 8, 2 * HD), f32),
        vmem((ny, 8, 2 * HD), f32),
        vmem((na, 8, 2 * HD), f32),
        vmem((ny, 8, 2 * HD), f32),
        vmem((nh, 16, lanes_w), bf16),
        vmem((nz, nh, 16, lanes_w), bf16),
        vmem((nx, tall_w, rows), bf16),
        vmem((nx, ny, tall_w, rows), bf16),
        vmem((nz, ny, wx, rows), bf16),
        vmem((ny, 2, piece, tokens), bf16),
        vmem((ny, 2, piece, tokens), bf16),
        vmem((2, piece, tokens), bf16),
        vmem((na, 2, piece, tokens), bf16),
        vmem((ny, 2, piece, tokens), bf16),
        vmem((2, tokens, rows), bf16),
        vmem((tokens, 2 * listed), jnp.int32),
        pltpu.SemaphoreType.DMA((6,)),
        pltpu.SemaphoreType.DMA((13, 16)),
        pltpu.SemaphoreType.DMA((13, 16)),
        pltpu.SemaphoreType.DMA((48,)),
        pltpu.SemaphoreType.DMA((48,)),
    ]
    in_vmem = pl.BlockSpec(memory_space=pltpu.VMEM)
    edges = pl.pallas_call(
        functools.partial(kernel, nz, ny, nx, nh, stop),
        out_shape=jax.ShapeDtypeStruct((2, 2 * listed, tokens), bf16),
        in_specs=[pl.BlockSpec(memory_space=pltpu.SMEM), in_vmem]
        + [pl.BlockSpec(memory_space=pl.ANY)] * 6,
        out_specs=in_vmem,
        scratch_shapes=scratch,
        compiler_params=pltpu.CompilerParams(
            collective_id=cid, has_side_effects=True, vmem_limit_bytes=60 * 1024 * 1024
        ),
    )(positions, grads, raw, out_proj, value_proj, decoders, ids, act)
    return edges.astype(f32).reshape(4, listed, tokens).transpose(0, 2, 1)


def solution(mesh, sizes=(NZ, NY, NX, NH), stop=99, cid=0):
    placed = (
        P("head", "feat"),
        P(),
        P("head", None, None),
        P("head", "feat"),
        P("head", "feat"),
        P("feat", None),
        P(),
        P(),
    )
    return jax.shard_map(
        functools.partial(body, *sizes, stop, cid),
        mesh=mesh,
        in_specs=placed,
        out_specs=P("head", None, None),
        check_vma=False,
    )
```

```python
import functools

import jax
import jax.numpy as jnp
from jax import lax
from jax.experimental import pallas as pl
from jax.experimental.pallas import tpu as pltpu
from jax.sharding import PartitionSpec as P

MESH = pl.DeviceIdType.MESH
HD = 128
NZ, NY, NX, NH = 2, 8, 4, 8
NT = (((1,), (1,)), ((), ()))


def dot(a, b, dims=(((1,), (0,)), ((), ()))):
    return lax.dot_general(a, b, dims, preferred_element_type=jnp.float32)


def kernel(
    nz, ny, nx, nh, stop,
    pos_ref, grads_ref, raw_hbm, outp_hbm, valp_hbm, dec_hbm, ids_hbm, act_hbm,
    out_ref,
    raw_ref, outp_ref, valp_ref, ids_ref, act_ref, dec, gall, ga, gy, gfull, pall, psend, part, rs, ex, hall, tsend, tall, ax, bx, thr,
    eparts, ers, e1, eex, fin, pats, ids_t,
    in_sem, ssem, rsem,
):
    f32, bf16 = jnp.float32, jnp.bfloat16
    na = nz * nx
    w = grads_ref.shape[1]
    wx = nx * w
    listed, tokens = ids_ref.shape
    feats = dec.shape[0]
    rows = nh * 16
    f = lax.axis_index("feat")
    g = lax.axis_index("head")
    x = lax.rem(f, nx)
    y = lax.rem(lax.div(f, nx), ny)
    z = lax.div(f, nx * ny)
    a = z * nx + x

    def place(dz, dy, dx, dh):
        zj, yj, xj = lax.rem(z + dz, nz), lax.rem(y + dy, ny), lax.rem(x + dx, nx)
        gj = lax.rem(g + dh, nh)
        return zj, yj, xj, gj, (zj * (nx * ny) + yj * nx + xj, gj)

    def far_first(n):
        return sorted(range(1, n), key=lambda d: -min(d, n - d))

    groups = {
        "h": [(d, place(0, 0, 0, d)) for d in far_first(nh)],
        "y": [(d, place(0, d, 0, 0)) for d in far_first(ny)],
        "x": [(d, place(0, 0, d, 0)) for d in far_first(nx)],
        "a": [(nx * k + d, place(k, 0, d, 0)) for k in range(1, nz) for d in far_first(nx) + [0]]
        + [(d, place(0, 0, d, 0)) for d in far_first(nx)],
        "zh": [(d, place(1, 0, 0, d)) for d in [0] + far_first(nh)[::-1]],
    }

    barrier = pltpu.get_barrier_semaphore()
    greet = groups["a"] + groups["y"] + groups["zh"][1:] + groups["h"]
    greet = [who for slot, who in greet]
    for who in greet:
        pl.semaphore_signal(barrier, inc=1, device_id=who[4], device_id_type=MESH)

    loads = {}
    for i, (name, src, dst) in enumerate(
        (
            ("raw", raw_hbm, raw_ref),
            ("outp", outp_hbm, outp_ref),
            ("valp", valp_hbm, valp_ref),
            ("ids", ids_hbm, ids_ref),
            ("act", act_hbm, act_ref),
            ("dec", dec_hbm, dec),
        )
    ):
        loads[name] = pltpu.make_async_copy(src, dst, in_sem.at[i])
        loads[name].start()

    def load(name):
        loads[name].wait()
        loaded.append(name)

    def exchange(stage, group, src, dst, whole, each=None):
        copies = {}
        for slot, who in groups[group]:
            copies[slot] = pltpu.make_async_remote_copy(
                src_ref=src(who),
                dst_ref=dst(slot),
                send_sem=ssem.at[stage],
                recv_sem=rsem.at[stage if each is None else each + slot],
                device_id=who[4],
                device_id_type=MESH,
            )
            copies[slot].start()
        sent.append((stage, whole))
        return copies if each is not None else (stage, whole)

    def send(sems, src, dst, device):
        copy = pltpu.make_async_remote_copy(
            src_ref=src,
            dst_ref=dst,
            send_sem=ssem.at[sems[0]],
            recv_sem=rsem.at[sems[1]],
            device_id=device,
            device_id_type=MESH,
        )
        copy.start()
        return copy

    def all_of(stage, whole):
        return pltpu.make_async_remote_copy(
            src_ref=whole,
            dst_ref=whole,
            send_sem=ssem.at[stage],
            recv_sem=rsem.at[stage],
            device_id=groups["h"][0][1][4],
            device_id_type=MESH,
        )

    def arrive(one):
        all_of(*one).wait_recv()

    def finish():
        for one in sent:
            all_of(*one).wait_send()
        for name, copy in loads.items():
            if name not in loaded:
                copy.wait()

    sent, loaded = [], []

    own = grads_ref[...].astype(f32)
    mine = jnp.concatenate([own, own], axis=0)
    zero_lanes = jnp.zeros((8, gall.shape[2]), f32)
    gall[g] = zero_lanes
    gall[g, :, 0:w] = mine
    ga[a] = zero_lanes
    ga[a, :, 0:w] = mine
    pl.semaphore_wait(barrier, len(greet))
    c0 = exchange(0, "h", lambda j: gall.at[g], lambda d: gall.at[g], gall.at[0 : nh - 1])

    load("raw")
    for j in range(nh):
        for h in range(4):
            psend[j, 4 * h : 4 * h + 4, :] = raw_ref[h, 4 * j : 4 * j + 4, :]
    tsend[...] = jnp.zeros_like(tsend)
    gfull[...] = jnp.zeros_like(gfull)
    load("outp")

    arrive(c0)
    if stop <= 0:
        return finish()
    both = gall[...].reshape(nh * 8, gall.shape[2])[:, 0:w]
    low = lax.rem(lax.broadcasted_iota(jnp.int32, both.shape, 0), 8) < 4
    half = 2 * HD
    partial = dot(jnp.where(low, both, 0.0).astype(bf16), outp_ref[:, 0:half])
    partial += dot(jnp.where(low, 0.0, both).astype(bf16), outp_ref[:, half : 2 * half])
    part[...] = partial.reshape(ny, 8, half)
    c4 = exchange(4, "y", lambda who: part.at[who[1]], lambda d: rs.at[d], rs.at[0 : ny - 1])
    c2 = exchange(2, "a", lambda j: ga.at[a], lambda d: ga.at[a], ga.at[0 : na - 1])

    arrive(c4)
    if stop <= 4:
        return finish()
    total = part[y]
    for d in range(1, ny):
        total += rs[d]
    ex[0] = total
    c5 = exchange(5, "a", lambda j: ex.at[0], lambda d: ex.at[d], ex.at[0 : na - 1])

    arrive(c2)
    for k in range(nz):
        for i in range(nx):
            gy[y, 4 * k : 4 * k + 4, w * i : w * i + w] = ga[k * nx + i, 0:4, 0:w]
    c3 = exchange(3, "y", lambda j: gy.at[y], lambda d: gy.at[y], gy.at[0 : ny - 1])

    r = lax.broadcasted_iota(jnp.int32, (rows, ny * 8), 0)
    c = lax.broadcasted_iota(jnp.int32, (rows, ny * 8), 1)
    from_row = lax.div(r, 16) * 8 + lax.div(lax.rem(r, 16), 8) * 4 + lax.rem(r, 4)
    choose = (c == from_row).astype(bf16)
    r = lax.broadcasted_iota(jnp.int32, (rows, half), 0)
    lane = lax.broadcasted_iota(jnp.int32, (rows, half), 1)
    fits = lax.rem(lax.div(r, 4), 2) == lax.div(lane, HD)
    upper = lax.rem(lax.div(r, 8), 2) == 1

    arrive(c5)
    if stop <= 5:
        return finish()
    for d in range(1, na):
        total += ex[d]
    hall[y] = total.astype(bf16).astype(f32)
    c6 = exchange(6, "y", lambda j: hall.at[y], lambda d: hall.at[y], hall.at[0 : ny - 1])

    arrive(c6)
    if stop <= 6:
        return finish()
    hin = hall[...].reshape(ny * 8, half).astype(bf16)
    spread = dot(choose, hin)
    first = jnp.where(fits & ~upper, spread, 0.0).astype(bf16)
    second = jnp.where(fits & upper, spread, 0.0).astype(bf16)
    load("valp")
    through = dot(first, valp_ref[:, 0:half], NT)
    through += dot(second, valp_ref[:, half : 2 * half], NT)
    tsend[:, :, 0:w] = through.astype(bf16).reshape(nh, 16, w)
    c7 = exchange(7, "zh", lambda who: tsend.at[who[3]], lambda d: tall.at[z, g], tall.at[0])
    c13 = exchange(
        13, "h", lambda who: tsend.at[who[3]], lambda d: tall.at[z, g], tall.at[0, 0 : nh - 1]
    )
    tall[z, g] = tsend[g]

    load("ids")
    load("act")
    ids = ids_ref[...] - f * feats
    ids_t[...] = jnp.concatenate([ids, ids], axis=0).T

    arrive(c13)
    arrive(c7)
    if stop <= 7:
        return finish()
    tall_w = ax.shape[1]

    def turned(k):
        block = tall[k].reshape(rows, tall.shape[3]).astype(f32).T
        return block[0:tall_w].astype(bf16)

    ax[x] = turned(0)
    cx = exchange(8, "x", lambda j: ax.at[x], lambda d: ax.at[x], ax.at[0 : nx - 1])
    bx[x, 0] = turned(1)
    cy = exchange(9, "y", lambda j: bx.at[x, 0], lambda d: bx.at[x, d], bx.at[0, 0 : ny - 1], 24)
    right, left = place(0, 0, 1, 0)[4], place(0, 0, nx - 1, 0)[4]
    from_left, from_right = lax.rem(x + nx - 1, nx), lax.rem(x + 1, nx)

    def y_at(d):
        who = place(0, d, 0, 0)
        return who[1], who[4]

    hops = {}
    reach = ny // 2

    def pass_on(d):
        sems = (14, 32 + d if d < reach else 14)
        hops["r", d] = send(sems, bx.at[x, d], bx.at[x, d], right)
        sems = (15, 32 + d if d >= reach else 15)
        hops["l", d] = send(sems, bx.at[x, d], bx.at[x, d], left)

    pass_on(0)
    arrive(cx)
    joined = [ax[i].astype(f32)[0:w] for i in range(nx)]
    thr[0, y] = jnp.concatenate(joined, axis=0).astype(bf16)
    mine_y = thr.at[0, y]
    far = {}
    steps = (2, ny - 2, 1, ny - 1) if ny == 8 else (1,)
    for i, d in enumerate(steps):
        far[d] = send((18, 19 + i if i < 2 and ny == 8 else 18), mine_y, mine_y, y_at(d)[1])
    order = (1, ny - 1, 2, ny - 2, 3, ny - 3, 4) if ny == 8 else (1,)
    for d in order:
        cy[d].wait_recv()
        pass_on(d)
    c1 = exchange(1, "h", lambda who: psend.at[who[3]], lambda d: pall.at[g], pall.at[0 : nh - 1])
    pall[g] = psend[g]

    load("dec")
    arrive(c3)
    for k in range(nz):
        for j in range(ny):
            at = wx * (k * ny + j)
            gfull[0:4, at : at + wx] = gy[j, 4 * k : 4 * k + 4, 0:wx]

    cut = (wx // 32) * 16
    if ny == 8:
        far[2].wait_recv()
        back = thr.at[0, y_at(ny - 2)[0]]
        far[3] = send((18, 18), back, back, y_at(1)[1])
        back = thr.at[0, y_at(ny - 2)[0], 0:cut]
        far["low"] = send((18, 18), back, back, y_at(2)[1])
        far[ny - 2].wait_recv()
        back = thr.at[0, y_at(2)[0]]
        far[ny - 3] = send((18, 18), back, back, y_at(ny - 1)[1])
        back = thr.at[0, y_at(2)[0], cut:wx]
        far["high"] = send((18, 18), back, back, y_at(ny - 2)[1])
    for d in (0,) + order:
        if d < reach:
            hops["r", d].wait_recv()
            send((16, 16), bx.at[from_left, d], bx.at[from_left, d], right)
        else:
            hops["l", d].wait_recv()
            send((16, 17), bx.at[from_right, d], bx.at[from_right, d], left)

    arrive(c1)
    raw = pall[...].reshape(rows, tokens)
    row_t = lax.rem(lax.broadcasted_iota(jnp.int32, raw.shape, 0), 4)
    spot = lax.broadcasted_iota(jnp.int32, raw.shape, 1)
    row_pos = jnp.zeros(raw.shape, jnp.int32)
    own_pos = []
    for t in range(4):
        own_pos.append(pos_ref[4 * g + t])
        row_pos = jnp.where(row_t == t, own_pos[t], row_pos)
    masked = jnp.where(spot <= row_pos, raw, 0.0)
    pattern = masked / jnp.sum(masked, axis=1, keepdims=True)
    pat = pattern.T
    pat_hi = pat.astype(bf16)
    pat_lo = (pat - pat_hi.astype(f32)).astype(bf16)
    pats[0] = pat_hi
    pats[1] = pat_lo

    straight = dot(gfull[...].astype(bf16), dec[...], NT)

    sent.append((18, thr.at[0, 0 : ny - 1]))
    arrive((18, thr.at[0, 0 : ny - 3] if ny == 8 else thr.at[0, 0 : ny - 1]))
    span = ny * wx
    scores = dot(dec[:, 0:span], thr[0].reshape(span, rows))
    sent.extend([(14, bx.at[0]), (15, bx.at[0]), (16, bx.at[0])])
    arrive((14, bx.at[0, 0 : ny - reach]))
    arrive((15, bx.at[0, 0:reach]))
    for lane_way, first_d, last_d in ((16, 0, reach), (17, reach, ny)):
        arrive((lane_way, bx.at[0, first_d:last_d]))
        if stop > 9:
            for d in range(first_d, last_d):
                joined = [bx[i, d].astype(f32)[0:w] for i in range(nx)]
                thr[1, y_at(ny - d)[0]] = jnp.concatenate(joined, axis=0).astype(bf16)
    if stop <= 9:
        return finish()
    scores += dot(dec[:, span : 2 * span], thr[1].reshape(span, rows))
    sc_hi = scores.astype(bf16)
    sc_lo = (scores - sc_hi.astype(f32)).astype(bf16)
    right = jnp.concatenate([sc_hi, sc_hi, sc_lo], axis=1)

    ids = ids_t[...]
    act = act_ref[...]
    act = jnp.concatenate([act, act], axis=0)
    lane = lax.broadcasted_iota(jnp.int32, ids.shape, 1)
    pat_hi, pat_lo = pats[0], pats[1]
    of_t = lax.rem(lax.broadcasted_iota(jnp.int32, pat_hi.shape, 1), 4)
    token = lax.broadcasted_iota(jnp.int32, (tokens, feats), 0)
    piece = 2 * listed // ny
    for p in range(2):
        picked = []
        for q in range(2):
            t = 2 * p + q
            hi = jnp.where(of_t == t, pat_hi, 0.0)
            lo = jnp.where(of_t == t, pat_lo, 0.0)
            left = jnp.concatenate([hi, lo, hi], axis=1)
            table = dot(left, right, NT)
            table += jnp.where(token == own_pos[t], straight[t : t + 1, :], 0.0)
            found = jnp.zeros(ids.shape, f32)
            for b in range(feats // 128):
                local = ids - 128 * b
                inside = (local >= 0) & (local < 128)
                taken = jnp.take_along_axis(
                    table[:, 128 * b : 128 * b + 128], jnp.clip(local, 0, 127), axis=1
                )
                found = jnp.where(inside, taken, found)
            picked.append(found)
        edge = jnp.where(lane < listed, picked[0], picked[1]).T * act
        edge = edge.astype(bf16)
        for j in range(ny):
            eparts[j, p] = edge[piece * j : piece * (j + 1)]

    c10 = exchange(10, "y", lambda who: eparts.at[who[1]], lambda d: ers.at[d], ers.at[0 : ny - 1])
    arrive(c10)
    if stop <= 10:
        return finish()
    total = eparts[y].astype(f32)
    for d in range(1, ny):
        total += ers[d].astype(f32)
    e1[...] = total.astype(bf16)
    c11 = exchange(11, "a", lambda j: e1, lambda d: eex.at[d], eex.at[0 : na - 1])
    arrive(c11)
    if stop <= 11:
        return finish()
    for d in range(1, na):
        total += eex[d].astype(f32)
    fin[y] = total.astype(bf16)
    c12 = exchange(12, "y", lambda j: fin.at[y], lambda d: fin.at[y], fin.at[0 : ny - 1])
    arrive(c12)
    if stop <= 12:
        return finish()
    for j in range(ny):
        for p in range(2):
            out_ref[p, piece * j : piece * (j + 1), :] = fin[j, p]

    finish()


def body(nz, ny, nx, nh, stop, cid, grads, positions, raw, out_proj, value_proj, decoders, ids, act):
    f32, bf16 = jnp.float32, jnp.bfloat16
    out_proj, value_proj, ids, act = out_proj.T, value_proj.T, ids.T, act.T
    w = grads.shape[1]
    listed, tokens = ids.shape
    feats, width = decoders.shape
    na, rows, piece = nz * nx, nh * 16, 2 * listed // ny
    wx = nx * w
    lanes_w = -(-w // 128) * 128
    lanes_x = -(-wx // 128) * 128
    tall_w = -(-w // 16) * 16
    vmem = pltpu.VMEM
    scratch = [
        vmem(raw.shape, f32),
        vmem(out_proj.shape, bf16),
        vmem(value_proj.shape, bf16),
        vmem(ids.shape, jnp.int32),
        vmem(act.shape, f32),
        vmem((feats, width), bf16),
        vmem((nh, 8, lanes_w), f32),
        vmem((na, 8, lanes_w), f32),
        vmem((ny, 8, lanes_x), f32),
        vmem((8, width), f32),
        vmem((nh, 16, tokens), f32),
        vmem((nh, 16, tokens), f32),
        vmem((ny, 8, 2 * HD), f32),
        vmem((ny, 8, 2 * HD), f32),
        vmem((na, 8, 2 * HD), f32),
        vmem((ny, 8, 2 * HD), f32),
        vmem((nh, 16, lanes_w), bf16),
        vmem((nz, nh, 16, lanes_w), bf16),
        vmem((nx, tall_w, rows), bf16),
        vmem((nx, ny, tall_w, rows), bf16),
        vmem((nz, ny, wx, rows), bf16),
        vmem((ny, 2, piece, tokens), bf16),
        vmem((ny, 2, piece, tokens), bf16),
        vmem((2, piece, tokens), bf16),
        vmem((na, 2, piece, tokens), bf16),
        vmem((ny, 2, piece, tokens), bf16),
        vmem((2, tokens, rows), bf16),
        vmem((tokens, 2 * listed), jnp.int32),
        pltpu.SemaphoreType.DMA((6,)),
        pltpu.SemaphoreType.DMA((19,)),
        pltpu.SemaphoreType.DMA((32 + ny,)),
    ]
    in_vmem = pl.BlockSpec(memory_space=pltpu.VMEM)
    edges = pl.pallas_call(
        functools.partial(kernel, nz, ny, nx, nh, stop),
        out_shape=jax.ShapeDtypeStruct((2, 2 * listed, tokens), bf16),
        in_specs=[pl.BlockSpec(memory_space=pltpu.SMEM), in_vmem]
        + [pl.BlockSpec(memory_space=pl.ANY)] * 6,
        out_specs=in_vmem,
        scratch_shapes=scratch,
        compiler_params=pltpu.CompilerParams(
            collective_id=cid, has_side_effects=True, vmem_limit_bytes=60 * 1024 * 1024
        ),
    )(positions, grads, raw, out_proj, value_proj, decoders, ids, act)
    return edges.astype(f32).reshape(4, listed, tokens).transpose(0, 2, 1)


def solution(mesh, sizes=(NZ, NY, NX, NH), stop=99, cid=0):
    placed = (
        P("head", "feat"),
        P(),
        P("head", None, None),
        P("head", "feat"),
        P("head", "feat"),
        P("feat", None),
        P(),
        P(),
    )
    return jax.shard_map(
        functools.partial(body, *sizes, stop, cid),
        mesh=mesh,
        in_specs=placed,
        out_specs=P("head", None, None),
        check_vma=False,
    )
```

```python
import functools

import jax
import jax.numpy as jnp
from jax import lax
from jax.experimental import pallas as pl
from jax.experimental.pallas import tpu as pltpu
from jax.sharding import PartitionSpec as P

MESH = pl.DeviceIdType.MESH
HD = 128
NZ, NY, NX, NH = 2, 8, 4, 8
NT = (((1,), (1,)), ((), ()))


def dot(a, b, dims=(((1,), (0,)), ((), ()))):
    return lax.dot_general(a, b, dims, preferred_element_type=jnp.float32)


def kernel(
    nz, ny, nx, nh, stop,
    pos_hbm, grads_hbm, raw_hbm, outp_hbm, valp_hbm, dec_hbm, ids_hbm, act_hbm,
    out_ref,
    pos_ref, grads_ref, raw_ref, outp_ref, valp_ref, ids_ref, act_ref, dec, gall, ga, gy, gfull, pall, psend, part, rs, ex, hall, tsend, tall, ax, bx, thr,
    eparts, ers, e1, eex, pats, ids_t,
    in_sem, ssem, rsem,
):
    f32, bf16 = jnp.float32, jnp.bfloat16
    na = nz * nx
    w = grads_ref.shape[1]
    wx = nx * w
    listed, tokens = ids_ref.shape
    feats = dec.shape[0]
    rows = nh * 16
    f = lax.axis_index("feat")
    g = lax.axis_index("head")
    x = lax.rem(f, nx)
    y = lax.rem(lax.div(f, nx), ny)
    z = lax.div(f, nx * ny)
    a = z * nx + x

    def place(dz, dy, dx, dh):
        zj, yj, xj = lax.rem(z + dz, nz), lax.rem(y + dy, ny), lax.rem(x + dx, nx)
        gj = lax.rem(g + dh, nh)
        return zj, yj, xj, gj, (zj * (nx * ny) + yj * nx + xj, gj)

    def far_first(n):
        return sorted(range(1, n), key=lambda d: -min(d, n - d))

    groups = {
        "h": [(d, place(0, 0, 0, d)) for d in far_first(nh)],
        "y": [(d, place(0, d, 0, 0)) for d in far_first(ny)],
        "x": [(d, place(0, 0, d, 0)) for d in far_first(nx)],
        "a": [(nx * k + d, place(k, 0, d, 0)) for k in range(1, nz) for d in far_first(nx) + [0]]
        + [(d, place(0, 0, d, 0)) for d in far_first(nx)],
        "zh": [(d, place(1, 0, 0, d)) for d in [0] + far_first(nh)[::-1]],
    }

    barrier = pltpu.get_barrier_semaphore()
    greet = groups["a"] + groups["y"] + groups["zh"][1:] + groups["h"]
    greet = [who for slot, who in greet]
    for who in greet:
        pl.semaphore_signal(barrier, inc=1, device_id=who[4], device_id_type=MESH)

    loads = {}
    for i, (name, src, dst) in enumerate(
        (
            ("grads", grads_hbm, grads_ref),
            ("raw", raw_hbm, raw_ref),
            ("outp", outp_hbm, outp_ref),
            ("valp", valp_hbm, valp_ref),
            ("ids", ids_hbm, ids_ref),
            ("act", act_hbm, act_ref),
            ("pos", pos_hbm, pos_ref),
            ("dec", dec_hbm, dec),
        )
    ):
        loads[name] = pltpu.make_async_copy(src, dst, in_sem.at[i])
        loads[name].start()

    def load(name):
        loads[name].wait()
        loaded.append(name)

    def exchange(stage, group, src, dst, whole, each=None):
        copies = {}
        for slot, who in groups[group]:
            copies[slot] = pltpu.make_async_remote_copy(
                src_ref=src(who),
                dst_ref=dst(slot),
                send_sem=ssem.at[stage],
                recv_sem=rsem.at[stage if each is None else each + slot],
                device_id=who[4],
                device_id_type=MESH,
            )
            copies[slot].start()
        sent.append((stage, whole))
        return copies if each is not None else (stage, whole)

    def send(sems, src, dst, device):
        copy = pltpu.make_async_remote_copy(
            src_ref=src,
            dst_ref=dst,
            send_sem=ssem.at[sems[0]],
            recv_sem=rsem.at[sems[1]],
            device_id=device,
            device_id_type=MESH,
        )
        copy.start()
        return copy

    def all_of(stage, whole):
        return pltpu.make_async_remote_copy(
            src_ref=whole,
            dst_ref=whole,
            send_sem=ssem.at[stage],
            recv_sem=rsem.at[stage],
            device_id=groups["h"][0][1][4],
            device_id_type=MESH,
        )

    def arrive(one):
        all_of(*one).wait_recv()

    def finish():
        for one in sent:
            all_of(*one).wait_send()
        for name, copy in loads.items():
            if name not in loaded:
                copy.wait()

    sent, loaded = [], []

    load("grads")
    own = grads_ref[...].astype(f32)
    mine = jnp.concatenate([own, own], axis=0)
    zero_lanes = jnp.zeros((8, gall.shape[2]), f32)
    gall[g] = zero_lanes
    gall[g, :, 0:w] = mine
    ga[a] = zero_lanes
    ga[a, :, 0:w] = mine
    pl.semaphore_wait(barrier, len(greet))
    c0 = exchange(0, "h", lambda j: gall.at[g], lambda d: gall.at[g], gall.at[0 : nh - 1])

    load("raw")
    for j in range(nh):
        for h in range(4):
            psend[j, 4 * h : 4 * h + 4, :] = raw_ref[h, 4 * j : 4 * j + 4, :]
    tsend[...] = jnp.zeros_like(tsend)
    gfull[...] = jnp.zeros_like(gfull)
    load("outp")

    arrive(c0)
    if stop <= 0:
        return finish()
    both = gall[...].reshape(nh * 8, gall.shape[2])[:, 0:w]
    low = lax.rem(lax.broadcasted_iota(jnp.int32, both.shape, 0), 8) < 4
    half = 2 * HD
    partial = dot(jnp.where(low, both, 0.0).astype(bf16), outp_ref[:, 0:half])
    partial += dot(jnp.where(low, 0.0, both).astype(bf16), outp_ref[:, half : 2 * half])
    part[...] = partial.reshape(ny, 8, half)
    c4 = exchange(4, "y", lambda who: part.at[who[1]], lambda d: rs.at[d], rs.at[0 : ny - 1])
    c1 = exchange(1, "h", lambda who: psend.at[who[3]], lambda d: pall.at[g], pall.at[0 : nh - 1])
    pall[g] = psend[g]
    c2 = exchange(2, "a", lambda j: ga.at[a], lambda d: ga.at[a], ga.at[0 : na - 1])

    arrive(c4)
    if stop <= 4:
        return finish()
    total = part[y]
    for d in range(1, ny):
        total += rs[d]
    ex[0] = total
    c5 = exchange(5, "a", lambda j: ex.at[0], lambda d: ex.at[d], ex.at[0 : na - 1])

    arrive(c2)
    for k in range(nz):
        for i in range(nx):
            gy[y, 4 * k : 4 * k + 4, w * i : w * i + w] = ga[k * nx + i, 0:4, 0:w]
    c3 = exchange(3, "y", lambda j: gy.at[y], lambda d: gy.at[y], gy.at[0 : ny - 1])

    r = lax.broadcasted_iota(jnp.int32, (rows, ny * 8), 0)
    c = lax.broadcasted_iota(jnp.int32, (rows, ny * 8), 1)
    from_row = lax.div(r, 16) * 8 + lax.div(lax.rem(r, 16), 8) * 4 + lax.rem(r, 4)
    choose = (c == from_row).astype(bf16)
    r = lax.broadcasted_iota(jnp.int32, (rows, half), 0)
    lane = lax.broadcasted_iota(jnp.int32, (rows, half), 1)
    fits = lax.rem(lax.div(r, 4), 2) == lax.div(lane, HD)
    upper = lax.rem(lax.div(r, 8), 2) == 1

    arrive(c5)
    if stop <= 5:
        return finish()
    for d in range(1, na):
        total += ex[d]
    hall[y] = total.astype(bf16).astype(f32)
    c6 = exchange(6, "y", lambda j: hall.at[y], lambda d: hall.at[y], hall.at[0 : ny - 1])

    arrive(c6)
    if stop <= 6:
        return finish()
    hin = hall[...].reshape(ny * 8, half).astype(bf16)
    spread = dot(choose, hin)
    first = jnp.where(fits & ~upper, spread, 0.0).astype(bf16)
    second = jnp.where(fits & upper, spread, 0.0).astype(bf16)
    load("valp")
    through = dot(first, valp_ref[:, 0:half], NT)
    through += dot(second, valp_ref[:, half : 2 * half], NT)
    tsend[:, :, 0:w] = through.astype(bf16).reshape(nh, 16, w)
    c7 = exchange(7, "zh", lambda who: tsend.at[who[3]], lambda d: tall.at[z, g], tall.at[0])
    c13 = exchange(
        13, "h", lambda who: tsend.at[who[3]], lambda d: tall.at[z, g], tall.at[0, 0 : nh - 1]
    )
    tall[z, g] = tsend[g]

    load("ids")
    load("act")
    ids = ids_ref[...] - f * feats
    ids_t[...] = jnp.concatenate([ids, ids], axis=0).T

    arrive(c13)
    arrive(c7)
    if stop <= 7:
        return finish()
    tall_w = ax.shape[1]

    def turned(k):
        block = tall[k].reshape(rows, tall.shape[3]).astype(f32).T
        return block[0:tall_w].astype(bf16)

    ax[x] = turned(0)
    cx = exchange(8, "x", lambda j: ax.at[x], lambda d: ax.at[x], ax.at[0 : nx - 1])
    bx[x, 0] = turned(1)
    cy = exchange(9, "y", lambda j: bx.at[x, 0], lambda d: bx.at[x, d], bx.at[0, 0 : ny - 1], 24)
    right, left = place(0, 0, 1, 0)[4], place(0, 0, nx - 1, 0)[4]
    from_left, from_right = lax.rem(x + nx - 1, nx), lax.rem(x + 1, nx)

    def y_at(d):
        who = place(0, d, 0, 0)
        return who[1], who[4]

    hops = {}
    reach = ny // 2

    def pass_on(d):
        sems = (14, 32 + d if d < reach else 14)
        hops["r", d] = send(sems, bx.at[x, d], bx.at[x, d], right)
        sems = (15, 32 + d if d >= reach else 15)
        hops["l", d] = send(sems, bx.at[x, d], bx.at[x, d], left)

    pass_on(0)
    arrive(cx)
    joined = [ax[i].astype(f32)[0:w] for i in range(nx)]
    thr[0, y] = jnp.concatenate(joined, axis=0).astype(bf16)
    mine_y = thr.at[0, y]
    far = {}
    steps = (2, ny - 2, 1, ny - 1) if ny == 8 else (1,)
    for i, d in enumerate(steps):
        far[d] = send((22, 23 + i if i < 2 and ny == 8 else 22), mine_y, mine_y, y_at(d)[1])
    order = (1, ny - 1, 2, ny - 2, 3, ny - 3, 4) if ny == 8 else (1,)
    for d in order:
        cy[d].wait_recv()
        pass_on(d)

    load("dec")
    arrive(c3)
    for k in range(nz):
        for j in range(ny):
            at = wx * (k * ny + j)
            gfull[0:4, at : at + wx] = gy[j, 4 * k : 4 * k + 4, 0:wx]

    arrive(c1)
    raw = pall[...].reshape(rows, tokens)
    row_t = lax.rem(lax.broadcasted_iota(jnp.int32, raw.shape, 0), 4)
    spot = lax.broadcasted_iota(jnp.int32, raw.shape, 1)
    row_pos = jnp.zeros(raw.shape, jnp.int32)
    own_pos = []
    for t in range(4):
        if t == 0:
            load("pos")
        own_pos.append(pos_ref[4 * g + t])
        row_pos = jnp.where(row_t == t, own_pos[t], row_pos)
    masked = jnp.where(spot <= row_pos, raw, 0.0)
    pattern = masked / jnp.sum(masked, axis=1, keepdims=True)
    pat = pattern.T
    pat_hi = pat.astype(bf16)
    pat_lo = (pat - pat_hi.astype(f32)).astype(bf16)
    pats[0] = pat_hi
    pats[1] = pat_lo

    cut = (wx // 32) * 16
    if ny == 8:
        far[2].wait_recv()
        back = thr.at[0, y_at(ny - 2)[0]]
        far[3] = send((22, 22), back, back, y_at(1)[1])
        back = thr.at[0, y_at(ny - 2)[0], 0:cut]
        far["low"] = send((22, 22), back, back, y_at(2)[1])
        far[ny - 2].wait_recv()
        back = thr.at[0, y_at(2)[0]]
        far[ny - 3] = send((22, 22), back, back, y_at(ny - 1)[1])
        back = thr.at[0, y_at(2)[0], cut:wx]
        far["high"] = send((22, 22), back, back, y_at(ny - 2)[1])
    for d in (0,) + order:
        if d < reach:
            hops["r", d].wait_recv()
            send((16, 16), bx.at[from_left, d], bx.at[from_left, d], right)
        else:
            hops["l", d].wait_recv()
            send((16, 17), bx.at[from_right, d], bx.at[from_right, d], left)

    straight = dot(gfull[...].astype(bf16), dec[...], NT)

    sent.append((22, thr.at[0, 0 : ny - 1]))
    arrive((22, thr.at[0, 0 : ny - 3] if ny == 8 else thr.at[0, 0 : ny - 1]))
    span = ny * wx
    scores = dot(dec[:, 0:span], thr[0].reshape(span, rows))
    sent.extend([(14, bx.at[0]), (15, bx.at[0]), (16, bx.at[0])])
    arrive((14, bx.at[0, 0 : ny - reach]))
    arrive((15, bx.at[0, 0:reach]))
    for lane_way, first_d, last_d in ((16, 0, reach), (17, reach, ny)):
        arrive((lane_way, bx.at[0, first_d:last_d]))
        if stop > 9:
            for d in range(first_d, last_d):
                joined = [bx[i, d].astype(f32)[0:w] for i in range(nx)]
                thr[1, y_at(ny - d)[0]] = jnp.concatenate(joined, axis=0).astype(bf16)
    if stop <= 9:
        return finish()
    scores += dot(dec[:, span : 2 * span], thr[1].reshape(span, rows))
    sc_hi = scores.astype(bf16)
    sc_lo = (scores - sc_hi.astype(f32)).astype(bf16)
    right = jnp.concatenate([sc_hi, sc_hi, sc_lo], axis=1)

    ids = ids_t[...]
    act = act_ref[...]
    act = jnp.concatenate([act, act], axis=0)
    lane = lax.broadcasted_iota(jnp.int32, ids.shape, 1)
    pat_hi, pat_lo = pats[0], pats[1]
    of_t = lax.rem(lax.broadcasted_iota(jnp.int32, pat_hi.shape, 1), 4)
    token = lax.broadcasted_iota(jnp.int32, (tokens, feats), 0)
    piece = 2 * listed // ny
    summed, spread_out, placed = {}, {}, {}
    for p in range(2):
        picked = []
        for q in range(2):
            t = 2 * p + q
            hi = jnp.where(of_t == t, pat_hi, 0.0)
            lo = jnp.where(of_t == t, pat_lo, 0.0)
            left = jnp.concatenate([hi, lo, hi], axis=1)
            table = dot(left, right, NT)
            table += jnp.where(token == own_pos[t], straight[t : t + 1, :], 0.0)
            found = jnp.zeros(ids.shape, f32)
            for b in range(feats // 128):
                local = ids - 128 * b
                inside = (local >= 0) & (local < 128)
                taken = jnp.take_along_axis(
                    table[:, 128 * b : 128 * b + 128], jnp.clip(local, 0, 127), axis=1
                )
                found = jnp.where(inside, taken, found)
            picked.append(found)
        edge = jnp.where(lane < listed, picked[0], picked[1]).T * act
        edge = edge.astype(bf16)
        for j in range(ny):
            eparts[p, j] = edge[piece * j : piece * (j + 1)]
        summed[p] = exchange(
            10 if p == 0 else 19,
            "y",
            lambda who: eparts.at[p, who[1]],
            lambda d: ers.at[p, d],
            ers.at[p, 0 : ny - 1],
        )

    totals = {}
    for p in range(2):
        arrive(summed[p])
        if stop <= 10 and p == 1:
            return finish()
        total = eparts[p, y].astype(f32)
        for d in range(1, ny):
            total += ers[p, d].astype(f32)
        totals[p] = total
        eex[p, 0] = total.astype(bf16)
        spread_out[p] = exchange(
            11 if p == 0 else 20,
            "a",
            lambda who: eex.at[p, 0],
            lambda d: eex.at[p, d],
            eex.at[p, 0 : na - 1],
        )
    keep = {}
    for p in range(2):
        arrive(spread_out[p])
        total = totals[p]
        for d in range(1, na):
            total += eex[p, d].astype(f32)
        e1[p] = total.astype(bf16)
        mine_out = out_ref.at[p, pl.ds(pl.multiple_of(y * piece, piece), piece), :]
        placed[p] = exchange(
            12 if p == 0 else 21,
            "y",
            lambda who: e1.at[p],
            lambda d: mine_out,
            ers.at[p, 0 : ny - 1],
        )
        keep[p] = pltpu.make_async_copy(e1.at[p], mine_out, in_sem.at[p])
        keep[p].start()
    for p in range(2):
        arrive(placed[p])
        keep[p].wait()
    finish()


def body(nz, ny, nx, nh, stop, cid, grads, positions, raw, out_proj, value_proj, decoders, ids, act):
    f32, bf16 = jnp.float32, jnp.bfloat16
    out_proj, value_proj, ids, act = out_proj.T, value_proj.T, ids.T, act.T
    w = grads.shape[1]
    listed, tokens = ids.shape
    feats, width = decoders.shape
    na, rows, piece = nz * nx, nh * 16, 2 * listed // ny
    wx = nx * w
    lanes_w = -(-w // 128) * 128
    lanes_x = -(-wx // 128) * 128
    tall_w = -(-w // 16) * 16
    vmem = pltpu.VMEM
    scratch = [
        pltpu.SMEM(positions.shape, jnp.int32),
        vmem(grads.shape, bf16),
        vmem(raw.shape, f32),
        vmem(out_proj.shape, bf16),
        vmem(value_proj.shape, bf16),
        vmem(ids.shape, jnp.int32),
        vmem(act.shape, f32),
        vmem((feats, width), bf16),
        vmem((nh, 8, lanes_w), f32),
        vmem((na, 8, lanes_w), f32),
        vmem((ny, 8, lanes_x), f32),
        vmem((8, width), f32),
        vmem((nh, 16, tokens), f32),
        vmem((nh, 16, tokens), f32),
        vmem((ny, 8, 2 * HD), f32),
        vmem((ny, 8, 2 * HD), f32),
        vmem((na, 8, 2 * HD), f32),
        vmem((ny, 8, 2 * HD), f32),
        vmem((nh, 16, lanes_w), bf16),
        vmem((nz, nh, 16, lanes_w), bf16),
        vmem((nx, tall_w, rows), bf16),
        vmem((nx, ny, tall_w, rows), bf16),
        vmem((nz, ny, wx, rows), bf16),
        vmem((2, ny, piece, tokens), bf16),
        vmem((2, ny, piece, tokens), bf16),
        vmem((2, piece, tokens), bf16),
        vmem((2, na, piece, tokens), bf16),
        vmem((2, tokens, rows), bf16),
        vmem((tokens, 2 * listed), jnp.int32),
        pltpu.SemaphoreType.DMA((8,)),
        pltpu.SemaphoreType.DMA((23,)),
        pltpu.SemaphoreType.DMA((32 + ny,)),
    ]
    edges = pl.pallas_call(
        functools.partial(kernel, nz, ny, nx, nh, stop),
        out_shape=jax.ShapeDtypeStruct((2, 2 * listed, tokens), bf16),
        in_specs=[pl.BlockSpec(memory_space=pl.ANY)] * 8,
        out_specs=pl.BlockSpec(memory_space=pl.ANY),
        scratch_shapes=scratch,
        compiler_params=pltpu.CompilerParams(
            collective_id=cid, has_side_effects=True, vmem_limit_bytes=60 * 1024 * 1024
        ),
    )(positions, grads, raw, out_proj, value_proj, decoders, ids, act)
    return edges.astype(f32).reshape(4, listed, tokens).transpose(0, 2, 1)


def solution(mesh, sizes=(NZ, NY, NX, NH), stop=99, cid=0):
    placed = (
        P("head", "feat"),
        P(),
        P("head", None, None),
        P("head", "feat"),
        P("head", "feat"),
        P("feat", None),
        P(),
        P(),
    )
    return jax.shard_map(
        functools.partial(body, *sizes, stop, cid),
        mesh=mesh,
        in_specs=placed,
        out_specs=P("head", None, None),
        check_vma=False,
    )
```

```python
import functools

import jax
import jax.numpy as jnp
from jax import lax
from jax.experimental import pallas as pl
from jax.experimental.pallas import tpu as pltpu
from jax.sharding import PartitionSpec as P

MESH = pl.DeviceIdType.MESH
HD = 128
NZ, NY, NX, NH = 2, 8, 4, 8
NT = (((1,), (1,)), ((), ()))


def dot(a, b, dims=(((1,), (0,)), ((), ()))):
    return lax.dot_general(a, b, dims, preferred_element_type=jnp.float32)


def kernel(
    nz, ny, nx, nh, stop,
    pos_hbm, grads_hbm, raw_hbm, outp_hbm, valp_hbm, dec_hbm, ids_hbm, act_hbm,
    out_ref,
    pos_ref, grads_ref, raw_ref, outp_ref, valp_ref, ids_ref, act_ref, dec, gall, ga, gy, gfull, pall, psend, part, rs, ex, hall, tsend, tall, ax, bx, thr,
    eparts, ers, e1, eex, pats, ids_t,
    in_sem, ssem, rsem,
):
    f32, bf16 = jnp.float32, jnp.bfloat16
    na = nz * nx
    w = grads_ref.shape[1]
    wx = nx * w
    listed, tokens = ids_ref.shape
    feats = dec.shape[0]
    rows = nh * 16
    f = lax.axis_index("feat")
    g = lax.axis_index("head")
    x = lax.rem(f, nx)
    y = lax.rem(lax.div(f, nx), ny)
    z = lax.div(f, nx * ny)
    a = z * nx + x

    def place(dz, dy, dx, dh):
        zj, yj, xj = lax.rem(z + dz, nz), lax.rem(y + dy, ny), lax.rem(x + dx, nx)
        gj = lax.rem(g + dh, nh)
        return zj, yj, xj, gj, (zj * (nx * ny) + yj * nx + xj, gj)

    def far_first(n):
        return sorted(range(1, n), key=lambda d: -min(d, n - d))

    groups = {
        "h": [(d, place(0, 0, 0, d)) for d in far_first(nh)],
        "y": [(d, place(0, d, 0, 0)) for d in far_first(ny)],
        "x": [(d, place(0, 0, d, 0)) for d in far_first(nx)],
        "a": [(nx * k + d, place(k, 0, d, 0)) for k in range(1, nz) for d in far_first(nx) + [0]]
        + [(d, place(0, 0, d, 0)) for d in far_first(nx)],
        "zh": [(d, place(1, 0, 0, d)) for d in [0] + far_first(nh)[::-1]],
    }

    barrier = pltpu.get_barrier_semaphore()
    greet = groups["a"] + groups["y"] + groups["zh"][1:] + groups["h"]
    greet = [who for slot, who in greet]
    for who in greet:
        pl.semaphore_signal(barrier, inc=1, device_id=who[4], device_id_type=MESH)

    loads = {}
    for i, (name, src, dst) in enumerate(
        (
            ("grads", grads_hbm, grads_ref),
            ("raw", raw_hbm, raw_ref),
            ("outp", outp_hbm, outp_ref),
            ("valp", valp_hbm, valp_ref),
            ("ids", ids_hbm, ids_ref),
            ("act", act_hbm, act_ref),
            ("pos", pos_hbm, pos_ref),
            ("dec", dec_hbm, dec),
        )
    ):
        loads[name] = pltpu.make_async_copy(src, dst, in_sem.at[i])
        loads[name].start()

    def load(name):
        loads[name].wait()
        loaded.append(name)

    def exchange(stage, group, src, dst, whole, each=None):
        copies = {}
        for slot, who in groups[group]:
            copies[slot] = pltpu.make_async_remote_copy(
                src_ref=src(who),
                dst_ref=dst(slot),
                send_sem=ssem.at[stage],
                recv_sem=rsem.at[stage if each is None else each + slot],
                device_id=who[4],
                device_id_type=MESH,
            )
            copies[slot].start()
        sent.append((stage, whole))
        return copies if each is not None else (stage, whole)

    def send(sems, src, dst, device):
        copy = pltpu.make_async_remote_copy(
            src_ref=src,
            dst_ref=dst,
            send_sem=ssem.at[sems[0]],
            recv_sem=rsem.at[sems[1]],
            device_id=device,
            device_id_type=MESH,
        )
        copy.start()
        return copy

    def all_of(stage, whole):
        return pltpu.make_async_remote_copy(
            src_ref=whole,
            dst_ref=whole,
            send_sem=ssem.at[stage],
            recv_sem=rsem.at[stage],
            device_id=groups["h"][0][1][4],
            device_id_type=MESH,
        )

    def arrive(one):
        all_of(*one).wait_recv()

    def finish():
        for one in sent:
            all_of(*one).wait_send()
        for name, copy in loads.items():
            if name not in loaded:
                copy.wait()

    sent, loaded = [], []

    load("grads")
    own = grads_ref[...].astype(f32)
    mine = jnp.concatenate([own, own], axis=0)
    zero_lanes = jnp.zeros((8, gall.shape[2]), f32)
    gall[g] = zero_lanes
    gall[g, :, 0:w] = mine
    ga[a] = zero_lanes
    ga[a, :, 0:w] = mine
    pl.semaphore_wait(barrier, len(greet))
    c0 = exchange(0, "h", lambda j: gall.at[g], lambda d: gall.at[g], gall.at[0 : nh - 1])

    load("raw")
    for j in range(nh):
        for h in range(4):
            psend[j, 4 * h : 4 * h + 4, :] = raw_ref[h, 4 * j : 4 * j + 4, :]
    tsend[...] = jnp.zeros_like(tsend)
    gfull[...] = jnp.zeros_like(gfull)
    load("outp")

    arrive(c0)
    if stop <= 0:
        return finish()
    both = gall[...].reshape(nh * 8, gall.shape[2])[:, 0:w]
    low = lax.rem(lax.broadcasted_iota(jnp.int32, both.shape, 0), 8) < 4
    half = 2 * HD
    partial = dot(jnp.where(low, both, 0.0).astype(bf16), outp_ref[:, 0:half])
    partial += dot(jnp.where(low, 0.0, both).astype(bf16), outp_ref[:, half : 2 * half])
    part[...] = partial.reshape(ny, 8, half)
    c4 = exchange(4, "y", lambda who: part.at[who[1]], lambda d: rs.at[d], rs.at[0 : ny - 1])
    c1 = exchange(1, "h", lambda who: psend.at[who[3]], lambda d: pall.at[g], pall.at[0 : nh - 1])
    pall[g] = psend[g]
    c2 = exchange(2, "a", lambda j: ga.at[a], lambda d: ga.at[a], ga.at[0 : na - 1])

    arrive(c4)
    if stop <= 4:
        return finish()
    total = part[y]
    for d in range(1, ny):
        total += rs[d]
    ex[0] = total
    c5 = exchange(5, "a", lambda j: ex.at[0], lambda d: ex.at[d], ex.at[0 : na - 1])

    arrive(c2)
    for k in range(nz):
        for i in range(nx):
            gy[y, 4 * k : 4 * k + 4, w * i : w * i + w] = ga[k * nx + i, 0:4, 0:w]
    c3 = exchange(3, "y", lambda j: gy.at[y], lambda d: gy.at[y], gy.at[0 : ny - 1])

    r = lax.broadcasted_iota(jnp.int32, (rows, ny * 8), 0)
    c = lax.broadcasted_iota(jnp.int32, (rows, ny * 8), 1)
    from_row = lax.div(r, 16) * 8 + lax.div(lax.rem(r, 16), 8) * 4 + lax.rem(r, 4)
    choose = (c == from_row).astype(bf16)
    r = lax.broadcasted_iota(jnp.int32, (rows, half), 0)
    lane = lax.broadcasted_iota(jnp.int32, (rows, half), 1)
    fits = lax.rem(lax.div(r, 4), 2) == lax.div(lane, HD)
    upper = lax.rem(lax.div(r, 8), 2) == 1

    arrive(c5)
    if stop <= 5:
        return finish()
    for d in range(1, na):
        total += ex[d]
    hall[y] = total.astype(bf16).astype(f32)
    c6 = exchange(6, "y", lambda j: hall.at[y], lambda d: hall.at[y], hall.at[0 : ny - 1])

    arrive(c6)
    if stop <= 6:
        return finish()
    hin = hall[...].reshape(ny * 8, half).astype(bf16)
    spread = dot(choose, hin)
    first = jnp.where(fits & ~upper, spread, 0.0).astype(bf16)
    second = jnp.where(fits & upper, spread, 0.0).astype(bf16)
    load("valp")
    through = dot(first, valp_ref[:, 0:half], NT)
    through += dot(second, valp_ref[:, half : 2 * half], NT)
    tsend[:, :, 0:w] = through.astype(bf16).reshape(nh, 16, w)
    c7 = exchange(7, "zh", lambda who: tsend.at[who[3]], lambda d: tall.at[z, g], tall.at[0])
    c13 = exchange(
        13, "h", lambda who: tsend.at[who[3]], lambda d: tall.at[z, g], tall.at[0, 0 : nh - 1]
    )
    tall[z, g] = tsend[g]

    load("ids")
    load("act")
    ids = ids_ref[...] - f * feats
    ids_t[...] = jnp.concatenate([ids, ids], axis=0).T

    arrive(c13)
    arrive(c7)
    if stop <= 7:
        return finish()
    tall_w = ax.shape[1]

    def turned(k):
        block = tall[k].reshape(rows, tall.shape[3]).astype(f32).T
        return block[0:tall_w].astype(bf16)

    ax[x] = turned(0)
    cx = exchange(8, "x", lambda j: ax.at[x], lambda d: ax.at[x], ax.at[0 : nx - 1])
    bx[x, 0] = turned(1)
    cy = exchange(9, "y", lambda j: bx.at[x, 0], lambda d: bx.at[x, d], bx.at[0, 0 : ny - 1], 24)
    right, left = place(0, 0, 1, 0)[4], place(0, 0, nx - 1, 0)[4]
    from_left, from_right = lax.rem(x + nx - 1, nx), lax.rem(x + 1, nx)

    def y_at(d):
        who = place(0, d, 0, 0)
        return who[1], who[4]

    hops = {}
    reach = ny // 2

    def pass_on(d):
        sems = (14, 32 + d if d < reach else 14)
        hops["r", d] = send(sems, bx.at[x, d], bx.at[x, d], right)
        sems = (15, 32 + d if d >= reach else 15)
        hops["l", d] = send(sems, bx.at[x, d], bx.at[x, d], left)

    pass_on(0)
    arrive(cx)
    joined = [ax[i].astype(f32)[0:w] for i in range(nx)]
    thr[0, y] = jnp.concatenate(joined, axis=0).astype(bf16)
    mine_y = thr.at[0, y]
    far = {}
    steps = (2, ny - 2, 1, ny - 1) if ny == 8 else (1,)
    for i, d in enumerate(steps):
        far[d] = send((22, 23 + i if i < 2 and ny == 8 else 22), mine_y, mine_y, y_at(d)[1])
    order = (1, ny - 1, 2, ny - 2, 3, ny - 3, 4) if ny == 8 else (1,)
    for d in order:
        cy[d].wait_recv()
        pass_on(d)

    load("dec")
    arrive(c3)
    for k in range(nz):
        for j in range(ny):
            at = wx * (k * ny + j)
            gfull[0:4, at : at + wx] = gy[j, 4 * k : 4 * k + 4, 0:wx]

    arrive(c1)
    raw = pall[...].reshape(rows, tokens)
    row_t = lax.rem(lax.broadcasted_iota(jnp.int32, raw.shape, 0), 4)
    spot = lax.broadcasted_iota(jnp.int32, raw.shape, 1)
    row_pos = jnp.zeros(raw.shape, jnp.int32)
    own_pos = []
    for t in range(4):
        if t == 0:
            load("pos")
        own_pos.append(pos_ref[4 * g + t])
        row_pos = jnp.where(row_t == t, own_pos[t], row_pos)
    masked = jnp.where(spot <= row_pos, raw, 0.0)
    pattern = masked / jnp.sum(masked, axis=1, keepdims=True)
    pat = pattern.T
    pat_hi = pat.astype(bf16)
    pat_lo = (pat - pat_hi.astype(f32)).astype(bf16)
    pats[0] = pat_hi
    pats[1] = pat_lo

    cut = (wx // 32) * 16
    if ny == 8:
        far[2].wait_recv()
        back = thr.at[0, y_at(ny - 2)[0]]
        far[3] = send((22, 22), back, back, y_at(1)[1])
        back = thr.at[0, y_at(ny - 2)[0], 0:cut]
        far["low"] = send((22, 22), back, back, y_at(2)[1])
        far[ny - 2].wait_recv()
        back = thr.at[0, y_at(2)[0]]
        far[ny - 3] = send((22, 22), back, back, y_at(ny - 1)[1])
        back = thr.at[0, y_at(2)[0], cut:wx]
        far["high"] = send((22, 22), back, back, y_at(ny - 2)[1])
    for d in (0,) + order:
        if d < reach:
            hops["r", d].wait_recv()
            send((16, 16), bx.at[from_left, d], bx.at[from_left, d], right)
        else:
            hops["l", d].wait_recv()
            send((16, 17), bx.at[from_right, d], bx.at[from_right, d], left)

    straight = dot(gfull[...].astype(bf16), dec[...], NT)

    span = ny * wx
    sent.extend([(14, bx.at[0]), (15, bx.at[0]), (16, bx.at[0])])
    arrive((14, bx.at[0, 0 : ny - reach]))
    arrive((15, bx.at[0, 0:reach]))
    for lane_way, first_d, last_d in ((16, 0, reach), (17, reach, ny)):
        arrive((lane_way, bx.at[0, first_d:last_d]))
        for d in range(first_d, last_d):
            joined = [bx[i, d].astype(f32)[0:w] for i in range(nx)]
            thr[1, y_at(ny - d)[0]] = jnp.concatenate(joined, axis=0).astype(bf16)
    scores = dot(dec[:, span : 2 * span], thr[1].reshape(span, rows))
    sent.append((22, thr.at[0, 0 : ny - 1]))
    arrive((22, thr.at[0, 0 : ny - 3] if ny == 8 else thr.at[0, 0 : ny - 1]))
    if stop <= 9:
        return finish()
    scores += dot(dec[:, 0:span], thr[0].reshape(span, rows))
    sc_hi = scores.astype(bf16)
    sc_lo = (scores - sc_hi.astype(f32)).astype(bf16)
    right = jnp.concatenate([sc_hi, sc_hi, sc_lo], axis=1)

    ids = ids_t[...]
    act = act_ref[...]
    act = jnp.concatenate([act, act], axis=0)
    lane = lax.broadcasted_iota(jnp.int32, ids.shape, 1)
    pat_hi, pat_lo = pats[0], pats[1]
    of_t = lax.rem(lax.broadcasted_iota(jnp.int32, pat_hi.shape, 1), 4)
    token = lax.broadcasted_iota(jnp.int32, (tokens, feats), 0)
    piece = 2 * listed // ny
    summed, spread_out, placed = {}, {}, {}
    for p in range(2):
        picked = []
        for q in range(2):
            t = 2 * p + q
            hi = jnp.where(of_t == t, pat_hi, 0.0)
            lo = jnp.where(of_t == t, pat_lo, 0.0)
            left = jnp.concatenate([hi, lo, hi], axis=1)
            table = dot(left, right, NT)
            table += jnp.where(token == own_pos[t], straight[t : t + 1, :], 0.0)
            found = jnp.zeros(ids.shape, f32)
            for b in range(feats // 128):
                local = ids - 128 * b
                inside = (local >= 0) & (local < 128)
                taken = jnp.take_along_axis(
                    table[:, 128 * b : 128 * b + 128], jnp.clip(local, 0, 127), axis=1
                )
                found = jnp.where(inside, taken, found)
            picked.append(found)
        edge = jnp.where(lane < listed, picked[0], picked[1]).T * act
        edge = edge.astype(bf16)
        for j in range(ny):
            eparts[p, j] = edge[piece * j : piece * (j + 1)]
        summed[p] = exchange(
            10 if p == 0 else 19,
            "y",
            lambda who: eparts.at[p, who[1]],
            lambda d: ers.at[p, d],
            ers.at[p, 0 : ny - 1],
        )

    for p in range(2):
        arrive(summed[p])
        if stop <= 10 and p == 1:
            return finish()
        total = eparts[p, y]
        for d in range(1, ny):
            total += ers[p, d]
        eex[p, 0] = total
        spread_out[p] = exchange(
            11 if p == 0 else 20,
            "a",
            lambda who: eex.at[p, 0],
            lambda d: eex.at[p, d],
            eex.at[p, 0 : na - 1],
        )
    keep = {}
    for p in range(2):
        arrive(spread_out[p])
        total = eex[p, 0]
        for d in range(1, na):
            total += eex[p, d]
        e1[p] = total
        mine_out = out_ref.at[p, pl.ds(pl.multiple_of(y * piece, piece), piece), :]
        placed[p] = exchange(
            12 if p == 0 else 21,
            "y",
            lambda who: e1.at[p],
            lambda d: mine_out,
            ers.at[p, 0 : ny - 1],
        )
        keep[p] = pltpu.make_async_copy(e1.at[p], mine_out, in_sem.at[p])
        keep[p].start()
    for p in range(2):
        arrive(placed[p])
        keep[p].wait()
    finish()


def body(nz, ny, nx, nh, stop, cid, grads, positions, raw, out_proj, value_proj, decoders, ids, act):
    f32, bf16 = jnp.float32, jnp.bfloat16
    out_proj, value_proj, ids, act = out_proj.T, value_proj.T, ids.T, act.T
    w = grads.shape[1]
    listed, tokens = ids.shape
    feats, width = decoders.shape
    na, rows, piece = nz * nx, nh * 16, 2 * listed // ny
    wx = nx * w
    lanes_w = -(-w // 128) * 128
    lanes_x = -(-wx // 128) * 128
    tall_w = -(-w // 16) * 16
    vmem = pltpu.VMEM
    scratch = [
        pltpu.SMEM(positions.shape, jnp.int32),
        vmem(grads.shape, bf16),
        vmem(raw.shape, f32),
        vmem(out_proj.shape, bf16),
        vmem(value_proj.shape, bf16),
        vmem(ids.shape, jnp.int32),
        vmem(act.shape, f32),
        vmem((feats, width), bf16),
        vmem((nh, 8, lanes_w), f32),
        vmem((na, 8, lanes_w), f32),
        vmem((ny, 8, lanes_x), f32),
        vmem((8, width), f32),
        vmem((nh, 16, tokens), f32),
        vmem((nh, 16, tokens), f32),
        vmem((ny, 8, 2 * HD), f32),
        vmem((ny, 8, 2 * HD), f32),
        vmem((na, 8, 2 * HD), f32),
        vmem((ny, 8, 2 * HD), f32),
        vmem((nh, 16, lanes_w), bf16),
        vmem((nz, nh, 16, lanes_w), bf16),
        vmem((nx, tall_w, rows), bf16),
        vmem((nx, ny, tall_w, rows), bf16),
        vmem((nz, ny, wx, rows), bf16),
        vmem((2, ny, piece, tokens), bf16),
        vmem((2, ny, piece, tokens), bf16),
        vmem((2, piece, tokens), bf16),
        vmem((2, na, piece, tokens), bf16),
        vmem((2, tokens, rows), bf16),
        vmem((tokens, 2 * listed), jnp.int32),
        pltpu.SemaphoreType.DMA((8,)),
        pltpu.SemaphoreType.DMA((23,)),
        pltpu.SemaphoreType.DMA((32 + ny,)),
    ]
    in_hbm = [
        pltpu.with_memory_space_constraint(array, pltpu.HBM)
        for array in (positions, grads, raw, out_proj, value_proj, decoders, ids, act)
    ]
    edges = pl.pallas_call(
        functools.partial(kernel, nz, ny, nx, nh, stop),
        out_shape=jax.ShapeDtypeStruct((2, 2 * listed, tokens), bf16),
        in_specs=[pl.BlockSpec(memory_space=pltpu.HBM)] * 8,
        out_specs=pl.BlockSpec(memory_space=pltpu.VMEM),
        scratch_shapes=scratch,
        compiler_params=pltpu.CompilerParams(
            collective_id=cid, has_side_effects=True, vmem_limit_bytes=24 * 1024 * 1024
        ),
    )(*in_hbm)
    return edges.astype(f32).reshape(4, listed, tokens).transpose(0, 2, 1)


def solution(mesh, sizes=(NZ, NY, NX, NH), stop=99, cid=0):
    placed = (
        P("head", "feat"),
        P(),
        P("head", None, None),
        P("head", "feat"),
        P("head", "feat"),
        P("feat", None),
        P(),
        P(),
    )
    return jax.shard_map(
        functools.partial(body, *sizes, stop, cid),
        mesh=mesh,
        in_specs=placed,
        out_specs=P("head", None, None),
        check_vma=False,
    )
```

```python
import functools

import jax
import jax.numpy as jnp
from jax import lax
from jax.experimental import pallas as pl
from jax.experimental.pallas import tpu as pltpu
from jax.sharding import PartitionSpec as P

MESH = pl.DeviceIdType.MESH
HD = 128
NZ, NY, NX, NH = 2, 8, 4, 8
NT = (((1,), (1,)), ((), ()))


def dot(a, b, dims=(((1,), (0,)), ((), ()))):
    return lax.dot_general(a, b, dims, preferred_element_type=jnp.float32)


def kernel(
    nz, ny, nx, nh, stop,
    pos_hbm, grads_hbm, raw_hbm, outp_hbm, valp_hbm, dec_hbm, ids_hbm, act_hbm,
    out_ref,
    pos_ref, grads_ref, raw_ref, outp_ref, valp_ref, ids_ref, act_ref, dec, gall, ga, gy, gfull, pall, psend, part, rs, ex, hall, tsend, tall, ax, bx, thr,
    eparts, ers, e1, eex, pats, ids_t,
    in_sem, ssem, rsem,
):
    f32, bf16 = jnp.float32, jnp.bfloat16
    na = nz * nx
    w = grads_ref.shape[1]
    wx = nx * w
    listed, tokens = ids_ref.shape
    feats = dec.shape[0]
    rows = nh * 16
    f = lax.axis_index("feat")
    g = lax.axis_index("head")
    x = lax.rem(f, nx)
    y = lax.rem(lax.div(f, nx), ny)
    z = lax.div(f, nx * ny)
    a = z * nx + x

    def place(dz, dy, dx, dh):
        zj, yj, xj = lax.rem(z + dz, nz), lax.rem(y + dy, ny), lax.rem(x + dx, nx)
        gj = lax.rem(g + dh, nh)
        return zj, yj, xj, gj, (zj * (nx * ny) + yj * nx + xj, gj)

    def far_first(n):
        return sorted(range(1, n), key=lambda d: -min(d, n - d))

    groups = {
        "h": [(d, place(0, 0, 0, d)) for d in far_first(nh)],
        "y": [(d, place(0, d, 0, 0)) for d in far_first(ny)],
        "x": [(d, place(0, 0, d, 0)) for d in far_first(nx)],
        "a": [(nx * k + d, place(k, 0, d, 0)) for k in range(1, nz) for d in far_first(nx) + [0]]
        + [(d, place(0, 0, d, 0)) for d in far_first(nx)],
        "zh": [(d, place(1, 0, 0, d)) for d in [0] + far_first(nh)[::-1]],
    }

    barrier = pltpu.get_barrier_semaphore()
    greet = groups["a"] + groups["y"] + groups["zh"][1:] + groups["h"]
    greet = [who for slot, who in greet]
    for who in greet:
        pl.semaphore_signal(barrier, inc=1, device_id=who[4], device_id_type=MESH)

    loads = {}
    for i, (name, src, dst) in enumerate(
        (
            ("grads", grads_hbm, grads_ref),
            ("raw", raw_hbm, raw_ref),
            ("outp", outp_hbm, outp_ref),
            ("valp", valp_hbm, valp_ref),
            ("ids", ids_hbm, ids_ref),
            ("act", act_hbm, act_ref),
            ("pos", pos_hbm, pos_ref),
            ("dec", dec_hbm, dec),
        )
    ):
        loads[name] = pltpu.make_async_copy(src, dst, in_sem.at[i])
        loads[name].start()

    def load(name):
        loads[name].wait()
        loaded.append(name)

    def exchange(stage, group, src, dst, whole, each=None):
        copies = {}
        for slot, who in groups[group]:
            copies[slot] = pltpu.make_async_remote_copy(
                src_ref=src(who),
                dst_ref=dst(slot),
                send_sem=ssem.at[stage],
                recv_sem=rsem.at[stage if each is None else each + slot],
                device_id=who[4],
                device_id_type=MESH,
            )
            copies[slot].start()
        sent.append((stage, whole))
        return copies if each is not None else (stage, whole)

    def send(sems, src, dst, device):
        copy = pltpu.make_async_remote_copy(
            src_ref=src,
            dst_ref=dst,
            send_sem=ssem.at[sems[0]],
            recv_sem=rsem.at[sems[1]],
            device_id=device,
            device_id_type=MESH,
        )
        copy.start()
        return copy

    def all_of(stage, whole):
        return pltpu.make_async_remote_copy(
            src_ref=whole,
            dst_ref=whole,
            send_sem=ssem.at[min(stage, 22)],
            recv_sem=rsem.at[stage],
            device_id=groups["h"][0][1][4],
            device_id_type=MESH,
        )

    def arrive(one):
        all_of(*one).wait_recv()

    def finish():
        for one in sent:
            all_of(*one).wait_send()
        for name, copy in loads.items():
            if name not in loaded:
                copy.wait()

    sent, loaded = [], []

    load("grads")
    own = grads_ref[...].astype(f32)
    mine = jnp.concatenate([own, own], axis=0)
    zero_lanes = jnp.zeros((8, gall.shape[2]), f32)
    gall[g] = zero_lanes
    gall[g, :, 0:w] = mine
    ga[a] = zero_lanes
    ga[a, :, 0:w] = mine
    pl.semaphore_wait(barrier, len(greet))
    c0 = exchange(0, "h", lambda j: gall.at[g], lambda d: gall.at[g], gall.at[0 : nh - 1])

    load("raw")
    for j in range(nh):
        for h in range(4):
            psend[j, 4 * h : 4 * h + 4, :] = raw_ref[h, 4 * j : 4 * j + 4, :]
    tsend[...] = jnp.zeros_like(tsend)
    gfull[...] = jnp.zeros_like(gfull)
    load("outp")

    arrive(c0)
    if stop <= 0:
        return finish()
    both = gall[...].reshape(nh * 8, gall.shape[2])[:, 0:w]
    low = lax.rem(lax.broadcasted_iota(jnp.int32, both.shape, 0), 8) < 4
    half = 2 * HD
    partial = dot(jnp.where(low, both, 0.0).astype(bf16), outp_ref[:, 0:half])
    partial += dot(jnp.where(low, 0.0, both).astype(bf16), outp_ref[:, half : 2 * half])
    part[...] = partial.reshape(ny, 8, half)
    c4 = exchange(4, "y", lambda who: part.at[who[1]], lambda d: rs.at[d], rs.at[0 : ny - 1])
    c1 = exchange(1, "h", lambda who: psend.at[who[3]], lambda d: pall.at[g], pall.at[0 : nh - 1])
    pall[g] = psend[g]
    c2 = exchange(2, "a", lambda j: ga.at[a], lambda d: ga.at[a], ga.at[0 : na - 1])

    arrive(c4)
    if stop <= 4:
        return finish()
    total = part[y]
    for d in range(1, ny):
        total += rs[d]
    ex[0] = total
    c5 = exchange(5, "a", lambda j: ex.at[0], lambda d: ex.at[d], ex.at[0 : na - 1])

    arrive(c2)
    for k in range(nz):
        for i in range(nx):
            gy[y, 4 * k : 4 * k + 4, w * i : w * i + w] = ga[k * nx + i, 0:4, 0:w]
    c3 = exchange(3, "y", lambda j: gy.at[y], lambda d: gy.at[y], gy.at[0 : ny - 1])

    r = lax.broadcasted_iota(jnp.int32, (rows, ny * 8), 0)
    c = lax.broadcasted_iota(jnp.int32, (rows, ny * 8), 1)
    from_row = lax.div(r, 16) * 8 + lax.div(lax.rem(r, 16), 8) * 4 + lax.rem(r, 4)
    choose = (c == from_row).astype(bf16)
    r = lax.broadcasted_iota(jnp.int32, (rows, half), 0)
    lane = lax.broadcasted_iota(jnp.int32, (rows, half), 1)
    fits = lax.rem(lax.div(r, 4), 2) == lax.div(lane, HD)
    upper = lax.rem(lax.div(r, 8), 2) == 1

    arrive(c5)
    if stop <= 5:
        return finish()
    for d in range(1, na):
        total += ex[d]
    hall[y] = total.astype(bf16).astype(f32)
    c6 = exchange(6, "y", lambda j: hall.at[y], lambda d: hall.at[y], hall.at[0 : ny - 1])

    arrive(c6)
    if stop <= 6:
        return finish()
    hin = hall[...].reshape(ny * 8, half).astype(bf16)
    spread = dot(choose, hin)
    first = jnp.where(fits & ~upper, spread, 0.0).astype(bf16)
    second = jnp.where(fits & upper, spread, 0.0).astype(bf16)
    load("valp")
    through = dot(first, valp_ref[:, 0:half], NT)
    through += dot(second, valp_ref[:, half : 2 * half], NT)
    tsend[:, :, 0:w] = through.astype(bf16).reshape(nh, 16, w)
    c7 = exchange(7, "zh", lambda who: tsend.at[who[3]], lambda d: tall.at[z, g], tall.at[0])
    c13 = exchange(
        13, "h", lambda who: tsend.at[who[3]], lambda d: tall.at[z, g], tall.at[0, 0 : nh - 1]
    )
    tall[z, g] = tsend[g]

    load("ids")
    load("act")
    ids = ids_ref[...] - f * feats
    ids_t[...] = jnp.concatenate([ids, ids], axis=0).T

    arrive(c13)
    arrive(c7)
    if stop <= 7:
        return finish()
    tall_w = ax.shape[1]

    def turned(k):
        block = tall[k].reshape(rows, tall.shape[3]).astype(f32).T
        return block[0:tall_w].astype(bf16)

    ax[x] = turned(0)
    cx = exchange(8, "x", lambda j: ax.at[x], lambda d: ax.at[x], ax.at[0 : nx - 1])
    bx[x, 0] = turned(1)
    right, left = place(0, 0, 1, 0)[4], place(0, 0, nx - 1, 0)[4]
    from_left, from_right = lax.rem(x + nx - 1, nx), lax.rem(x + 1, nx)

    def y_at(d):
        who = place(0, d, 0, 0)
        return who[1], who[4]

    steps = (2, ny - 2, 1, ny - 1) if ny == 8 else (1,)
    for d in steps:
        send((9, 24 + d), bx.at[x, 0], bx.at[x, d], y_at(d)[1])
    sent.append((9, bx.at[0, 0 : ny - 1]))
    hops = {}
    reach = ny // 2

    def pass_on(d):
        sems = (14, 32 + d if d < reach else 14)
        hops["r", d] = send(sems, bx.at[x, d], bx.at[x, d], right)
        sems = (15, 32 + d if d >= reach else 15)
        hops["l", d] = send(sems, bx.at[x, d], bx.at[x, d], left)

    pass_on(0)
    arrive(cx)
    joined = [ax[i].astype(f32)[0:w] for i in range(nx)]
    thr[0, y] = jnp.concatenate(joined, axis=0).astype(bf16)
    mine_y = thr.at[0, y]
    far = {}
    for i, d in enumerate(steps):
        far[d] = send((22, 23 + i if i < 2 and ny == 8 else 22), mine_y, mine_y, y_at(d)[1])
    order = (2, ny - 2, 1, ny - 1, 3, ny - 3, 4) if ny == 8 else (1,)
    mid = (tall_w // 32) * 16
    for d in order:
        arrive((24 + d, bx.at[0, d]))
        if d == 2 and ny == 8:
            send((9, 27), bx.at[x, 2], bx.at[x, 3], y_at(1)[1])
            send((9, 28), bx.at[x, 2, 0:mid], bx.at[x, 4, 0:mid], y_at(2)[1])
        if d == ny - 2 and ny == 8:
            send((9, 29), bx.at[x, 6], bx.at[x, 5], y_at(ny - 1)[1])
            send((9, 28), bx.at[x, 6, mid:tall_w], bx.at[x, 4, mid:tall_w], y_at(ny - 2)[1])
        pass_on(d)

    load("dec")
    arrive(c3)
    for k in range(nz):
        for j in range(ny):
            at = wx * (k * ny + j)
            gfull[0:4, at : at + wx] = gy[j, 4 * k : 4 * k + 4, 0:wx]

    arrive(c1)
    raw = pall[...].reshape(rows, tokens)
    row_t = lax.rem(lax.broadcasted_iota(jnp.int32, raw.shape, 0), 4)
    spot = lax.broadcasted_iota(jnp.int32, raw.shape, 1)
    row_pos = jnp.zeros(raw.shape, jnp.int32)
    own_pos = []
    for t in range(4):
        if t == 0:
            load("pos")
        own_pos.append(pos_ref[4 * g + t])
        row_pos = jnp.where(row_t == t, own_pos[t], row_pos)
    masked = jnp.where(spot <= row_pos, raw, 0.0)
    pattern = masked / jnp.sum(masked, axis=1, keepdims=True)
    pat = pattern.T
    pat_hi = pat.astype(bf16)
    pat_lo = (pat - pat_hi.astype(f32)).astype(bf16)
    pats[0] = pat_hi
    pats[1] = pat_lo

    cut = (wx // 32) * 16
    if ny == 8:
        far[2].wait_recv()
        back = thr.at[0, y_at(ny - 2)[0]]
        far[3] = send((22, 22), back, back, y_at(1)[1])
        back = thr.at[0, y_at(ny - 2)[0], 0:cut]
        far["low"] = send((22, 22), back, back, y_at(2)[1])
        far[ny - 2].wait_recv()
        back = thr.at[0, y_at(2)[0]]
        far[ny - 3] = send((22, 22), back, back, y_at(ny - 1)[1])
        back = thr.at[0, y_at(2)[0], cut:wx]
        far["high"] = send((22, 22), back, back, y_at(ny - 2)[1])
    for d in (0,) + order:
        if d < reach:
            hops["r", d].wait_recv()
            send((16, 16), bx.at[from_left, d], bx.at[from_left, d], right)
        else:
            hops["l", d].wait_recv()
            send((16, 17), bx.at[from_right, d], bx.at[from_right, d], left)

    straight = dot(gfull[...].astype(bf16), dec[...], NT)

    span = ny * wx
    sent.extend([(14, bx.at[0]), (15, bx.at[0]), (16, bx.at[0])])
    arrive((14, bx.at[0, 0 : ny - reach]))
    arrive((15, bx.at[0, 0:reach]))
    for lane_way, first_d, last_d in ((16, 0, reach), (17, reach, ny)):
        arrive((lane_way, bx.at[0, first_d:last_d]))
        for d in range(first_d, last_d):
            joined = [bx[i, d].astype(f32)[0:w] for i in range(nx)]
            thr[1, y_at(ny - d)[0]] = jnp.concatenate(joined, axis=0).astype(bf16)
    scores = dot(dec[:, span : 2 * span], thr[1].reshape(span, rows))
    sent.append((22, thr.at[0, 0 : ny - 1]))
    arrive((22, thr.at[0, 0 : ny - 3] if ny == 8 else thr.at[0, 0 : ny - 1]))
    if stop <= 9:
        return finish()
    scores += dot(dec[:, 0:span], thr[0].reshape(span, rows))
    sc_hi = scores.astype(bf16)
    sc_lo = (scores - sc_hi.astype(f32)).astype(bf16)
    right = jnp.concatenate([sc_hi, sc_hi, sc_lo], axis=1)

    ids = ids_t[...]
    act = act_ref[...]
    act = jnp.concatenate([act, act], axis=0)
    lane = lax.broadcasted_iota(jnp.int32, ids.shape, 1)
    pat_hi, pat_lo = pats[0], pats[1]
    of_t = lax.rem(lax.broadcasted_iota(jnp.int32, pat_hi.shape, 1), 4)
    token = lax.broadcasted_iota(jnp.int32, (tokens, feats), 0)
    piece = 2 * listed // ny
    summed, spread_out, placed = {}, {}, {}
    for p in range(2):
        picked = []
        for q in range(2):
            t = 2 * p + q
            hi = jnp.where(of_t == t, pat_hi, 0.0)
            lo = jnp.where(of_t == t, pat_lo, 0.0)
            left = jnp.concatenate([hi, lo, hi], axis=1)
            table = dot(left, right, NT)
            table += jnp.where(token == own_pos[t], straight[t : t + 1, :], 0.0)
            found = jnp.zeros(ids.shape, f32)
            for b in range(feats // 128):
                local = ids - 128 * b
                inside = (local >= 0) & (local < 128)
                taken = jnp.take_along_axis(
                    table[:, 128 * b : 128 * b + 128], jnp.clip(local, 0, 127), axis=1
                )
                found = jnp.where(inside, taken, found)
            picked.append(found)
        edge = jnp.where(lane < listed, picked[0], picked[1]).T * act
        edge = edge.astype(bf16)
        for j in range(ny):
            eparts[p, j] = edge[piece * j : piece * (j + 1)]
        summed[p] = exchange(
            10 if p == 0 else 19,
            "y",
            lambda who: eparts.at[p, who[1]],
            lambda d: ers.at[p, d],
            ers.at[p, 0 : ny - 1],
        )

    for p in range(2):
        arrive(summed[p])
        if stop <= 10 and p == 1:
            return finish()
        total = eparts[p, y]
        for d in range(1, ny):
            total += ers[p, d]
        eex[p, 0] = total
        spread_out[p] = exchange(
            11 if p == 0 else 20,
            "a",
            lambda who: eex.at[p, 0],
            lambda d: eex.at[p, d],
            eex.at[p, 0 : na - 1],
        )
    keep = {}
    for p in range(2):
        arrive(spread_out[p])
        total = eex[p, 0]
        for d in range(1, na):
            total += eex[p, d]
        e1[p] = total
        mine_out = out_ref.at[p, pl.ds(pl.multiple_of(y * piece, piece), piece), :]
        placed[p] = exchange(
            12 if p == 0 else 21,
            "y",
            lambda who: e1.at[p],
            lambda d: mine_out,
            ers.at[p, 0 : ny - 1],
        )
        keep[p] = pltpu.make_async_copy(e1.at[p], mine_out, in_sem.at[p])
        keep[p].start()
    for p in range(2):
        arrive(placed[p])
        keep[p].wait()
    finish()


def body(nz, ny, nx, nh, stop, cid, grads, positions, raw, out_proj, value_proj, decoders, ids, act):
    f32, bf16 = jnp.float32, jnp.bfloat16
    out_proj, value_proj, ids, act = out_proj.T, value_proj.T, ids.T, act.T
    w = grads.shape[1]
    listed, tokens = ids.shape
    feats, width = decoders.shape
    na, rows, piece = nz * nx, nh * 16, 2 * listed // ny
    wx = nx * w
    lanes_w = -(-w // 128) * 128
    lanes_x = -(-wx // 128) * 128
    tall_w = -(-w // 16) * 16
    vmem = pltpu.VMEM
    scratch = [
        pltpu.SMEM(positions.shape, jnp.int32),
        vmem(grads.shape, bf16),
        vmem(raw.shape, f32),
        vmem(out_proj.shape, bf16),
        vmem(value_proj.shape, bf16),
        vmem(ids.shape, jnp.int32),
        vmem(act.shape, f32),
        vmem((feats, width), bf16),
        vmem((nh, 8, lanes_w), f32),
        vmem((na, 8, lanes_w), f32),
        vmem((ny, 8, lanes_x), f32),
        vmem((8, width), f32),
        vmem((nh, 16, tokens), f32),
        vmem((nh, 16, tokens), f32),
        vmem((ny, 8, 2 * HD), f32),
        vmem((ny, 8, 2 * HD), f32),
        vmem((na, 8, 2 * HD), f32),
        vmem((ny, 8, 2 * HD), f32),
        vmem((nh, 16, lanes_w), bf16),
        vmem((nz, nh, 16, lanes_w), bf16),
        vmem((nx, tall_w, rows), bf16),
        vmem((nx, ny, tall_w, rows), bf16),
        vmem((nz, ny, wx, rows), bf16),
        vmem((2, ny, piece, tokens), bf16),
        vmem((2, ny, piece, tokens), bf16),
        vmem((2, piece, tokens), bf16),
        vmem((2, na, piece, tokens), bf16),
        vmem((2, tokens, rows), bf16),
        vmem((tokens, 2 * listed), jnp.int32),
        pltpu.SemaphoreType.DMA((8,)),
        pltpu.SemaphoreType.DMA((23,)),
        pltpu.SemaphoreType.DMA((32 + ny,)),
    ]
    in_hbm = [
        pltpu.with_memory_space_constraint(array, pltpu.HBM)
        for array in (positions, grads, raw, out_proj, value_proj, decoders, ids, act)
    ]
    edges = pl.pallas_call(
        functools.partial(kernel, nz, ny, nx, nh, stop),
        out_shape=jax.ShapeDtypeStruct((2, 2 * listed, tokens), bf16),
        in_specs=[pl.BlockSpec(memory_space=pltpu.HBM)] * 8,
        out_specs=pl.BlockSpec(memory_space=pltpu.VMEM),
        scratch_shapes=scratch,
        compiler_params=pltpu.CompilerParams(
            collective_id=cid, has_side_effects=True, vmem_limit_bytes=24 * 1024 * 1024
        ),
    )(*in_hbm)
    return edges.astype(f32).reshape(4, listed, tokens).transpose(0, 2, 1)


def solution(mesh, sizes=(NZ, NY, NX, NH), stop=99, cid=0):
    placed = (
        P("head", "feat"),
        P(),
        P("head", None, None),
        P("head", "feat"),
        P("head", "feat"),
        P("feat", None),
        P(),
        P(),
    )
    return jax.shard_map(
        functools.partial(body, *sizes, stop, cid),
        mesh=mesh,
        in_specs=placed,
        out_specs=P("head", None, None),
        check_vma=False,
    )
```

```python
import functools

import jax
import jax.numpy as jnp
from jax import lax
from jax.experimental import pallas as pl
from jax.experimental.pallas import tpu as pltpu
from jax.sharding import PartitionSpec as P

MESH = pl.DeviceIdType.MESH
HD = 128
NZ, NY, NX, NH = 2, 8, 4, 8
NT = (((1,), (1,)), ((), ()))


def dot(a, b, dims=(((1,), (0,)), ((), ()))):
    return lax.dot_general(a, b, dims, preferred_element_type=jnp.float32)


def kernel(
    nz, ny, nx, nh, stop,
    pos_hbm, grads_hbm, raw_hbm, outp_hbm, valp_hbm, dec_hbm, ids_hbm, act_hbm,
    out_ref,
    pos_ref, grads_ref, raw_ref, outp_ref, valp_ref, ids_ref, act_ref, dec, gall, ga, gy, gfull, pall, psend, part, rs, ex, hall, tsend, tall, ax, bx, thr,
    eparts, ers, e1, eex, pats, ids_t,
    in_sem, ssem, rsem,
):
    f32, bf16 = jnp.float32, jnp.bfloat16
    na = nz * nx
    w = grads_ref.shape[1]
    wx = nx * w
    listed, tokens = ids_ref.shape
    feats = dec.shape[0]
    rows = nh * 16
    f = lax.axis_index("feat")
    g = lax.axis_index("head")
    x = lax.rem(f, nx)
    y = lax.rem(lax.div(f, nx), ny)
    z = lax.div(f, nx * ny)
    a = z * nx + x

    def place(dz, dy, dx, dh):
        zj, yj, xj = lax.rem(z + dz, nz), lax.rem(y + dy, ny), lax.rem(x + dx, nx)
        gj = lax.rem(g + dh, nh)
        return zj, yj, xj, gj, (zj * (nx * ny) + yj * nx + xj, gj)

    def far_first(n):
        return sorted(range(1, n), key=lambda d: -min(d, n - d))

    groups = {
        "h": [(d, place(0, 0, 0, d)) for d in far_first(nh)],
        "y": [(d, place(0, d, 0, 0)) for d in far_first(ny)],
        "x": [(d, place(0, 0, d, 0)) for d in far_first(nx)],
        "a": [(nx * k + d, place(k, 0, d, 0)) for k in range(1, nz) for d in far_first(nx) + [0]]
        + [(d, place(0, 0, d, 0)) for d in far_first(nx)],
        "zh": [(d, place(1, 0, 0, d)) for d in [0] + far_first(nh)[::-1]],
    }

    barrier = pltpu.get_barrier_semaphore()
    greet = groups["a"] + groups["y"] + groups["zh"][1:] + groups["h"]
    greet = [who for slot, who in greet]
    for who in greet:
        pl.semaphore_signal(barrier, inc=1, device_id=who[4], device_id_type=MESH)

    loads = {}
    for i, (name, src, dst) in enumerate(
        (
            ("grads", grads_hbm, grads_ref),
            ("raw", raw_hbm, raw_ref),
            ("outp", outp_hbm, outp_ref),
            ("valp", valp_hbm, valp_ref),
            ("ids", ids_hbm, ids_ref),
            ("act", act_hbm, act_ref),
            ("pos", pos_hbm, pos_ref),
            ("dec", dec_hbm, dec),
        )
    ):
        loads[name] = pltpu.make_async_copy(src, dst, in_sem.at[i])
        loads[name].start()

    def load(name):
        loads[name].wait()
        loaded.append(name)

    def exchange(stage, group, src, dst, whole, each=None):
        copies = {}
        for slot, who in groups[group]:
            copies[slot] = pltpu.make_async_remote_copy(
                src_ref=src(who),
                dst_ref=dst(slot),
                send_sem=ssem.at[stage],
                recv_sem=rsem.at[stage if each is None else each + slot],
                device_id=who[4],
                device_id_type=MESH,
            )
            copies[slot].start()
        sent.append((stage, whole))
        return copies if each is not None else (stage, whole)

    def send(sems, src, dst, device):
        copy = pltpu.make_async_remote_copy(
            src_ref=src,
            dst_ref=dst,
            send_sem=ssem.at[sems[0]],
            recv_sem=rsem.at[sems[1]],
            device_id=device,
            device_id_type=MESH,
        )
        copy.start()
        return copy

    def all_of(stage, whole):
        return pltpu.make_async_remote_copy(
            src_ref=whole,
            dst_ref=whole,
            send_sem=ssem.at[stage],
            recv_sem=rsem.at[stage],
            device_id=groups["h"][0][1][4],
            device_id_type=MESH,
        )

    def arrive(one):
        all_of(*one).wait_recv()

    def finish():
        for one in sent:
            all_of(*one).wait_send()
        for name, copy in loads.items():
            if name not in loaded:
                copy.wait()

    sent, loaded = [], []

    load("grads")
    own = grads_ref[...].astype(f32)
    mine = jnp.concatenate([own, own], axis=0)
    zero_lanes = jnp.zeros((8, gall.shape[2]), f32)
    gall[g] = zero_lanes
    gall[g, :, 0:w] = mine
    ga[a] = zero_lanes
    ga[a, :, 0:w] = mine
    pl.semaphore_wait(barrier, len(greet))
    c0 = exchange(0, "h", lambda j: gall.at[g], lambda d: gall.at[g], gall.at[0 : nh - 1])

    load("raw")
    for j in range(nh):
        for h in range(4):
            psend[j, 4 * h : 4 * h + 4, :] = raw_ref[h, 4 * j : 4 * j + 4, :]
    tsend[...] = jnp.zeros_like(tsend)
    gfull[...] = jnp.zeros_like(gfull)
    load("outp")

    arrive(c0)
    if stop <= 0:
        return finish()
    both = gall[...].reshape(nh * 8, gall.shape[2])[:, 0:w]
    low = lax.rem(lax.broadcasted_iota(jnp.int32, both.shape, 0), 8) < 4
    half = 2 * HD
    partial = dot(jnp.where(low, both, 0.0).astype(bf16), outp_ref[:, 0:half])
    partial += dot(jnp.where(low, 0.0, both).astype(bf16), outp_ref[:, half : 2 * half])
    part[...] = partial.reshape(ny, 8, half)
    c4 = exchange(4, "y", lambda who: part.at[who[1]], lambda d: rs.at[d], rs.at[0 : ny - 1])
    c1 = exchange(1, "h", lambda who: psend.at[who[3]], lambda d: pall.at[g], pall.at[0 : nh - 1])
    pall[g] = psend[g]
    c2 = exchange(2, "a", lambda j: ga.at[a], lambda d: ga.at[a], ga.at[0 : na - 1])

    arrive(c4)
    if stop <= 4:
        return finish()
    total = part[y]
    for d in range(1, ny):
        total += rs[d]
    ex[0] = total
    c5 = exchange(5, "a", lambda j: ex.at[0], lambda d: ex.at[d], ex.at[0 : na - 1])

    arrive(c2)
    for k in range(nz):
        for i in range(nx):
            gy[y, 4 * k : 4 * k + 4, w * i : w * i + w] = ga[k * nx + i, 0:4, 0:w]
    c3 = exchange(3, "y", lambda j: gy.at[y], lambda d: gy.at[y], gy.at[0 : ny - 1])

    r = lax.broadcasted_iota(jnp.int32, (rows, ny * 8), 0)
    c = lax.broadcasted_iota(jnp.int32, (rows, ny * 8), 1)
    from_row = lax.div(r, 16) * 8 + lax.div(lax.rem(r, 16), 8) * 4 + lax.rem(r, 4)
    choose = (c == from_row).astype(bf16)
    r = lax.broadcasted_iota(jnp.int32, (rows, half), 0)
    lane = lax.broadcasted_iota(jnp.int32, (rows, half), 1)
    fits = lax.rem(lax.div(r, 4), 2) == lax.div(lane, HD)
    upper = lax.rem(lax.div(r, 8), 2) == 1

    arrive(c5)
    if stop <= 5:
        return finish()
    for d in range(1, na):
        total += ex[d]
    hall[y] = total.astype(bf16).astype(f32)
    c6 = exchange(6, "y", lambda j: hall.at[y], lambda d: hall.at[y], hall.at[0 : ny - 1])

    arrive(c6)
    if stop <= 6:
        return finish()
    hin = hall[...].reshape(ny * 8, half).astype(bf16)
    spread = dot(choose, hin)
    first = jnp.where(fits & ~upper, spread, 0.0).astype(bf16)
    second = jnp.where(fits & upper, spread, 0.0).astype(bf16)
    load("valp")
    through = dot(first, valp_ref[:, 0:half], NT)
    through += dot(second, valp_ref[:, half : 2 * half], NT)
    tsend[:, :, 0:w] = through.astype(bf16).reshape(nh, 16, w)
    c7 = exchange(7, "zh", lambda who: tsend.at[who[3]], lambda d: tall.at[z, g], tall.at[0])
    c13 = exchange(
        13, "h", lambda who: tsend.at[who[3]], lambda d: tall.at[z, g], tall.at[0, 0 : nh - 1]
    )
    tall[z, g] = tsend[g]

    load("ids")
    load("act")
    ids = ids_ref[...] - f * feats
    ids_t[...] = jnp.concatenate([ids, ids], axis=0).T

    arrive(c13)
    arrive(c7)
    if stop <= 7:
        return finish()
    tall_w = ax.shape[1]

    def turned(k):
        block = tall[k].reshape(rows, tall.shape[3]).astype(f32).T
        return block[0:tall_w].astype(bf16)

    ax[x] = turned(0)
    cx = exchange(8, "x", lambda j: ax.at[x], lambda d: ax.at[x], ax.at[0 : nx - 1])
    bx[x, 0] = turned(1)
    cy = exchange(9, "y", lambda j: bx.at[x, 0], lambda d: bx.at[x, d], bx.at[0, 0 : ny - 1], 24)
    def y_at(d):
        who = place(0, d, 0, 0)
        return who[1], who[4]

    early = (0, 1, ny - 1, 2) if ny == 8 else (0,)

    def pass_on(d):
        for slot, who in groups["x"]:
            send((14, 14 if d in early else 15), bx.at[x, d], bx.at[x, d], who[4])

    pass_on(0)
    arrive(cx)
    joined = [ax[i].astype(f32)[0:w] for i in range(nx)]
    thr[0, y] = jnp.concatenate(joined, axis=0).astype(bf16)
    mine_y = thr.at[0, y]
    far = {}
    steps = (2, ny - 2, 1, ny - 1) if ny == 8 else (1,)
    for i, d in enumerate(steps):
        far[d] = send((22, 23 + i if i < 2 and ny == 8 else 22), mine_y, mine_y, y_at(d)[1])
    order = (1, ny - 1, 2, ny - 2, 3, ny - 3, 4) if ny == 8 else (1,)
    for d in order:
        cy[d].wait_recv()
        pass_on(d)

    cut = (wx // 32) * 16
    if ny == 8:
        far[2].wait_recv()
        back = thr.at[0, y_at(ny - 2)[0]]
        far[3] = send((22, 22), back, back, y_at(1)[1])
        back = thr.at[0, y_at(ny - 2)[0], 0:cut]
        far["low"] = send((22, 22), back, back, y_at(2)[1])
        far[ny - 2].wait_recv()
        back = thr.at[0, y_at(2)[0]]
        far[ny - 3] = send((22, 22), back, back, y_at(ny - 1)[1])
        back = thr.at[0, y_at(2)[0], cut:wx]
        far["high"] = send((22, 22), back, back, y_at(ny - 2)[1])
    load("dec")
    arrive(c3)
    for k in range(nz):
        for j in range(ny):
            at = wx * (k * ny + j)
            gfull[0:4, at : at + wx] = gy[j, 4 * k : 4 * k + 4, 0:wx]

    arrive(c1)
    raw = pall[...].reshape(rows, tokens)
    row_t = lax.rem(lax.broadcasted_iota(jnp.int32, raw.shape, 0), 4)
    spot = lax.broadcasted_iota(jnp.int32, raw.shape, 1)
    row_pos = jnp.zeros(raw.shape, jnp.int32)
    own_pos = []
    for t in range(4):
        if t == 0:
            load("pos")
        own_pos.append(pos_ref[4 * g + t])
        row_pos = jnp.where(row_t == t, own_pos[t], row_pos)
    masked = jnp.where(spot <= row_pos, raw, 0.0)
    pattern = masked / jnp.sum(masked, axis=1, keepdims=True)
    pat = pattern.T
    pat_hi = pat.astype(bf16)
    pat_lo = (pat - pat_hi.astype(f32)).astype(bf16)
    pats[0] = pat_hi
    pats[1] = pat_lo

    straight = dot(gfull[...].astype(bf16), dec[...], NT)

    span = ny * wx
    sent.append((14, bx.at[0 : nx - 1]))
    late = [d for d in range(ny) if d not in early]
    for stage, ds in ((14, early), (15, late)):
        arrive((stage, bx.at[0 : nx - 1, 0 : len(ds)]))
        for d in ds:
            joined = [bx[i, d].astype(f32)[0:w] for i in range(nx)]
            thr[1, y_at(ny - d)[0]] = jnp.concatenate(joined, axis=0).astype(bf16)
    scores = dot(dec[:, span : 2 * span], thr[1].reshape(span, rows))
    sent.append((22, thr.at[0, 0 : ny - 1]))
    arrive((22, thr.at[0, 0 : ny - 3] if ny == 8 else thr.at[0, 0 : ny - 1]))
    if stop <= 9:
        return finish()
    scores += dot(dec[:, 0:span], thr[0].reshape(span, rows))
    sc_hi = scores.astype(bf16)
    sc_lo = (scores - sc_hi.astype(f32)).astype(bf16)
    right = jnp.concatenate([sc_hi, sc_hi, sc_lo], axis=1)

    ids = ids_t[...]
    act = act_ref[...]
    act = jnp.concatenate([act, act], axis=0)
    lane = lax.broadcasted_iota(jnp.int32, ids.shape, 1)
    pat_hi, pat_lo = pats[0], pats[1]
    of_t = lax.rem(lax.broadcasted_iota(jnp.int32, pat_hi.shape, 1), 4)
    token = lax.broadcasted_iota(jnp.int32, (tokens, feats), 0)
    piece = 2 * listed // ny
    summed, spread_out, placed = {}, {}, {}
    for p in range(2):
        picked = []
        for q in range(2):
            t = 2 * p + q
            hi = jnp.where(of_t == t, pat_hi, 0.0)
            lo = jnp.where(of_t == t, pat_lo, 0.0)
            left = jnp.concatenate([hi, lo, hi], axis=1)
            table = dot(left, right, NT)
            table += jnp.where(token == own_pos[t], straight[t : t + 1, :], 0.0)
            found = jnp.zeros(ids.shape, f32)
            for b in range(feats // 128):
                local = ids - 128 * b
                inside = (local >= 0) & (local < 128)
                taken = jnp.take_along_axis(
                    table[:, 128 * b : 128 * b + 128], jnp.clip(local, 0, 127), axis=1
                )
                found = jnp.where(inside, taken, found)
            picked.append(found)
        edge = jnp.where(lane < listed, picked[0], picked[1]).T * act
        edge = edge.astype(bf16)
        for j in range(ny):
            eparts[p, j] = edge[piece * j : piece * (j + 1)]
        summed[p] = exchange(
            10 if p == 0 else 19,
            "y",
            lambda who: eparts.at[p, who[1]],
            lambda d: ers.at[p, d],
            ers.at[p, 0 : ny - 1],
        )

    for p in range(2):
        arrive(summed[p])
        if stop <= 10 and p == 1:
            return finish()
        total = eparts[p, y]
        for d in range(1, ny):
            total += ers[p, d]
        eex[p, 0] = total
        spread_out[p] = exchange(
            11 if p == 0 else 20,
            "a",
            lambda who: eex.at[p, 0],
            lambda d: eex.at[p, d],
            eex.at[p, 0 : na - 1],
        )
    keep = {}
    for p in range(2):
        arrive(spread_out[p])
        total = eex[p, 0]
        for d in range(1, na):
            total += eex[p, d]
        e1[p] = total
        mine_out = out_ref.at[p, pl.ds(pl.multiple_of(y * piece, piece), piece), :]
        placed[p] = exchange(
            12 if p == 0 else 21,
            "y",
            lambda who: e1.at[p],
            lambda d: mine_out,
            ers.at[p, 0 : ny - 1],
        )
        keep[p] = pltpu.make_async_copy(e1.at[p], mine_out, in_sem.at[p])
        keep[p].start()
    for p in range(2):
        arrive(placed[p])
        keep[p].wait()
    finish()


def body(nz, ny, nx, nh, stop, cid, grads, positions, raw, out_proj, value_proj, decoders, ids, act):
    f32, bf16 = jnp.float32, jnp.bfloat16
    out_proj, value_proj, ids, act = out_proj.T, value_proj.T, ids.T, act.T
    w = grads.shape[1]
    listed, tokens = ids.shape
    feats, width = decoders.shape
    na, rows, piece = nz * nx, nh * 16, 2 * listed // ny
    wx = nx * w
    lanes_w = -(-w // 128) * 128
    lanes_x = -(-wx // 128) * 128
    tall_w = -(-w // 16) * 16
    vmem = pltpu.VMEM
    scratch = [
        pltpu.SMEM(positions.shape, jnp.int32),
        vmem(grads.shape, bf16),
        vmem(raw.shape, f32),
        vmem(out_proj.shape, bf16),
        vmem(value_proj.shape, bf16),
        vmem(ids.shape, jnp.int32),
        vmem(act.shape, f32),
        vmem((feats, width), bf16),
        vmem((nh, 8, lanes_w), f32),
        vmem((na, 8, lanes_w), f32),
        vmem((ny, 8, lanes_x), f32),
        vmem((8, width), f32),
        vmem((nh, 16, tokens), f32),
        vmem((nh, 16, tokens), f32),
        vmem((ny, 8, 2 * HD), f32),
        vmem((ny, 8, 2 * HD), f32),
        vmem((na, 8, 2 * HD), f32),
        vmem((ny, 8, 2 * HD), f32),
        vmem((nh, 16, lanes_w), bf16),
        vmem((nz, nh, 16, lanes_w), bf16),
        vmem((nx, tall_w, rows), bf16),
        vmem((nx, ny, tall_w, rows), bf16),
        vmem((nz, ny, wx, rows), bf16),
        vmem((2, ny, piece, tokens), bf16),
        vmem((2, ny, piece, tokens), bf16),
        vmem((2, piece, tokens), bf16),
        vmem((2, na, piece, tokens), bf16),
        vmem((2, tokens, rows), bf16),
        vmem((tokens, 2 * listed), jnp.int32),
        pltpu.SemaphoreType.DMA((8,)),
        pltpu.SemaphoreType.DMA((23,)),
        pltpu.SemaphoreType.DMA((32 + ny,)),
    ]
    in_hbm = [
        pltpu.with_memory_space_constraint(array, pltpu.HBM)
        for array in (positions, grads, raw, out_proj, value_proj, decoders, ids, act)
    ]
    edges = pl.pallas_call(
        functools.partial(kernel, nz, ny, nx, nh, stop),
        out_shape=jax.ShapeDtypeStruct((2, 2 * listed, tokens), bf16),
        in_specs=[pl.BlockSpec(memory_space=pltpu.HBM)] * 8,
        out_specs=pl.BlockSpec(memory_space=pltpu.VMEM),
        scratch_shapes=scratch,
        compiler_params=pltpu.CompilerParams(
            collective_id=cid, has_side_effects=True, vmem_limit_bytes=24 * 1024 * 1024
        ),
    )(*in_hbm)
    return edges.astype(f32).reshape(4, listed, tokens).transpose(0, 2, 1)


def solution(mesh, sizes=(NZ, NY, NX, NH), stop=99, cid=0):
    placed = (
        P("head", "feat"),
        P(),
        P("head", None, None),
        P("head", "feat"),
        P("head", "feat"),
        P("feat", None),
        P(),
        P(),
    )
    return jax.shard_map(
        functools.partial(body, *sizes, stop, cid),
        mesh=mesh,
        in_specs=placed,
        out_specs=P("head", None, None),
        check_vma=False,
    )
```

```python
import functools

import jax
import jax.numpy as jnp
from jax import lax
from jax.experimental import pallas as pl
from jax.experimental.pallas import tpu as pltpu
from jax.sharding import PartitionSpec as P

MESH = pl.DeviceIdType.MESH
HD = 128
NZ, NY, NX, NH = 2, 8, 4, 8
NT = (((1,), (1,)), ((), ()))


def dot(a, b, dims=(((1,), (0,)), ((), ()))):
    return lax.dot_general(a, b, dims, preferred_element_type=jnp.float32)


def kernel(
    nz, ny, nx, nh, stop,
    pos_hbm, grads_hbm, raw_hbm, outp_hbm, valp_hbm, dec_hbm, ids_hbm, act_hbm,
    out_ref,
    pos_ref, grads_ref, raw_ref, outp_ref, valp_ref, ids_ref, act_ref, dec, gall, ga, gy, gfull, pall, psend, part, rs, ex, hall, tsend, tall, ax, bx, thr,
    eparts, ers, e1, eex, pats, ids_t,
    in_sem, ssem, rsem,
):
    f32, bf16 = jnp.float32, jnp.bfloat16
    na = nz * nx
    w = grads_ref.shape[1]
    wx = nx * w
    listed, tokens = ids_ref.shape
    feats = dec.shape[0]
    rows = nh * 16
    f = lax.axis_index("feat")
    g = lax.axis_index("head")
    x = lax.rem(f, nx)
    y = lax.rem(lax.div(f, nx), ny)
    z = lax.div(f, nx * ny)
    a = z * nx + x

    def place(dz, dy, dx, dh):
        zj, yj, xj = lax.rem(z + dz, nz), lax.rem(y + dy, ny), lax.rem(x + dx, nx)
        gj = lax.rem(g + dh, nh)
        return zj, yj, xj, gj, (zj * (nx * ny) + yj * nx + xj, gj)

    def far_first(n):
        return sorted(range(1, n), key=lambda d: -min(d, n - d))

    groups = {
        "h": [(d, place(0, 0, 0, d)) for d in far_first(nh)],
        "y": [(d, place(0, d, 0, 0)) for d in far_first(ny)],
        "x": [(d, place(0, 0, d, 0)) for d in far_first(nx)],
        "a": [(nx * k + d, place(k, 0, d, 0)) for k in range(1, nz) for d in far_first(nx) + [0]]
        + [(d, place(0, 0, d, 0)) for d in far_first(nx)],
        "zh": [(d, place(1, 0, 0, d)) for d in [0] + far_first(nh)[::-1]],
    }

    barrier = pltpu.get_barrier_semaphore()
    greet = groups["a"] + groups["y"] + groups["zh"][1:] + groups["h"]
    greet = [who for slot, who in greet]
    loads = {}
    for i, (name, src, dst) in enumerate(
        (
            ("grads", grads_hbm, grads_ref),
            ("raw", raw_hbm, raw_ref),
            ("outp", outp_hbm, outp_ref),
            ("valp", valp_hbm, valp_ref),
            ("ids", ids_hbm, ids_ref),
            ("act", act_hbm, act_ref),
            ("pos", pos_hbm, pos_ref),
            ("dec", dec_hbm, dec),
        )
    ):
        loads[name] = pltpu.make_async_copy(src, dst, in_sem.at[i])
    loads["grads"].start()
    for who in greet:
        pl.semaphore_signal(barrier, inc=1, device_id=who[4], device_id_type=MESH)

    def load(name):
        loads[name].wait()
        loaded.append(name)

    def exchange(stage, group, src, dst, whole, each=None):
        copies = {}
        for slot, who in groups[group]:
            copies[slot] = pltpu.make_async_remote_copy(
                src_ref=src(who),
                dst_ref=dst(slot),
                send_sem=ssem.at[stage],
                recv_sem=rsem.at[stage if each is None else each + slot],
                device_id=who[4],
                device_id_type=MESH,
            )
            copies[slot].start()
        sent.append((stage, whole))
        return copies if each is not None else (stage, whole)

    def send(sems, src, dst, device):
        copy = pltpu.make_async_remote_copy(
            src_ref=src,
            dst_ref=dst,
            send_sem=ssem.at[sems[0]],
            recv_sem=rsem.at[sems[1]],
            device_id=device,
            device_id_type=MESH,
        )
        copy.start()
        return copy

    def all_of(stage, whole):
        return pltpu.make_async_remote_copy(
            src_ref=whole,
            dst_ref=whole,
            send_sem=ssem.at[stage],
            recv_sem=rsem.at[stage],
            device_id=groups["h"][0][1][4],
            device_id_type=MESH,
        )

    def arrive(one):
        all_of(*one).wait_recv()

    def finish():
        for one in sent:
            all_of(*one).wait_send()
        for name, copy in loads.items():
            if name not in loaded:
                copy.wait()

    sent, loaded = [], []

    load("grads")
    own = grads_ref[...].astype(f32)
    mine = jnp.concatenate([own, own], axis=0)
    zero_lanes = jnp.zeros((8, gall.shape[2]), f32)
    gall[g] = zero_lanes
    gall[g, :, 0:w] = mine
    ga[a] = zero_lanes
    ga[a, :, 0:w] = mine
    pl.semaphore_wait(barrier, len(greet))
    c0 = exchange(0, "h", lambda j: gall.at[g], lambda d: gall.at[g], gall.at[0 : nh - 1])

    for name in loads:
        if name != "grads":
            loads[name].start()

    load("raw")
    for j in range(nh):
        for h in range(4):
            psend[j, 4 * h : 4 * h + 4, :] = raw_ref[h, 4 * j : 4 * j + 4, :]
    tsend[...] = jnp.zeros_like(tsend)
    gfull[...] = jnp.zeros_like(gfull)
    load("outp")

    arrive(c0)
    if stop <= 0:
        return finish()
    both = gall[...].reshape(nh * 8, gall.shape[2])[:, 0:w]
    low = lax.rem(lax.broadcasted_iota(jnp.int32, both.shape, 0), 8) < 4
    half = 2 * HD
    partial = dot(jnp.where(low, both, 0.0).astype(bf16), outp_ref[:, 0:half])
    partial += dot(jnp.where(low, 0.0, both).astype(bf16), outp_ref[:, half : 2 * half])
    part[...] = partial.reshape(ny, 8, half)
    c4 = exchange(4, "y", lambda who: part.at[who[1]], lambda d: rs.at[d], rs.at[0 : ny - 1])
    c1 = exchange(1, "h", lambda who: psend.at[who[3]], lambda d: pall.at[g], pall.at[0 : nh - 1])
    pall[g] = psend[g]
    c2 = exchange(2, "a", lambda j: ga.at[a], lambda d: ga.at[a], ga.at[0 : na - 1])

    arrive(c4)
    if stop <= 4:
        return finish()
    total = part[y]
    for d in range(1, ny):
        total += rs[d]
    ex[0] = total
    c5 = exchange(5, "a", lambda j: ex.at[0], lambda d: ex.at[d], ex.at[0 : na - 1])

    arrive(c2)
    for k in range(nz):
        for i in range(nx):
            gy[y, 4 * k : 4 * k + 4, w * i : w * i + w] = ga[k * nx + i, 0:4, 0:w]
    c3 = exchange(3, "y", lambda j: gy.at[y], lambda d: gy.at[y], gy.at[0 : ny - 1])

    r = lax.broadcasted_iota(jnp.int32, (rows, ny * 8), 0)
    c = lax.broadcasted_iota(jnp.int32, (rows, ny * 8), 1)
    from_row = lax.div(r, 16) * 8 + lax.div(lax.rem(r, 16), 8) * 4 + lax.rem(r, 4)
    choose = (c == from_row).astype(bf16)
    r = lax.broadcasted_iota(jnp.int32, (rows, half), 0)
    lane = lax.broadcasted_iota(jnp.int32, (rows, half), 1)
    fits = lax.rem(lax.div(r, 4), 2) == lax.div(lane, HD)
    upper = lax.rem(lax.div(r, 8), 2) == 1

    arrive(c5)
    if stop <= 5:
        return finish()
    for d in range(1, na):
        total += ex[d]
    hall[y] = total.astype(bf16).astype(f32)
    c6 = exchange(6, "y", lambda j: hall.at[y], lambda d: hall.at[y], hall.at[0 : ny - 1])

    arrive(c6)
    if stop <= 6:
        return finish()
    hin = hall[...].reshape(ny * 8, half).astype(bf16)
    spread = dot(choose, hin)
    first = jnp.where(fits & ~upper, spread, 0.0).astype(bf16)
    second = jnp.where(fits & upper, spread, 0.0).astype(bf16)
    load("valp")
    through = dot(first, valp_ref[:, 0:half], NT)
    through += dot(second, valp_ref[:, half : 2 * half], NT)
    tsend[:, :, 0:w] = through.astype(bf16).reshape(nh, 16, w)
    c7 = exchange(7, "zh", lambda who: tsend.at[who[3]], lambda d: tall.at[z, g], tall.at[0])
    c13 = exchange(
        13, "h", lambda who: tsend.at[who[3]], lambda d: tall.at[z, g], tall.at[0, 0 : nh - 1]
    )
    tall[z, g] = tsend[g]

    load("ids")
    load("act")
    ids = ids_ref[...] - f * feats
    ids_t[...] = jnp.concatenate([ids, ids], axis=0).T

    arrive(c13)
    arrive(c7)
    if stop <= 7:
        return finish()
    tall_w = ax.shape[1]

    def turned(k):
        block = tall[k].reshape(rows, tall.shape[3]).astype(f32).T
        return block[0:tall_w].astype(bf16)

    ax[x] = turned(0)
    cx = exchange(8, "x", lambda j: ax.at[x], lambda d: ax.at[x], ax.at[0 : nx - 1])
    bx[x, 0] = turned(1)
    cy = exchange(9, "y", lambda j: bx.at[x, 0], lambda d: bx.at[x, d], bx.at[0, 0 : ny - 1], 24)
    def y_at(d):
        who = place(0, d, 0, 0)
        return who[1], who[4]

    early = (0, 1, ny - 1, 2) if ny == 8 else (0,)

    def pass_on(d):
        for slot, who in groups["x"]:
            send((14, 14 if d in early else 15), bx.at[x, d], bx.at[x, d], who[4])

    pass_on(0)
    arrive(cx)
    joined = [ax[i].astype(f32)[0:w] for i in range(nx)]
    thr[0, y] = jnp.concatenate(joined, axis=0).astype(bf16)
    mine_y = thr.at[0, y]
    far = {}
    steps = (2, ny - 2, 1, ny - 1) if ny == 8 else (1,)
    for i, d in enumerate(steps):
        far[d] = send((22, 23 + i if i < 2 and ny == 8 else 22), mine_y, mine_y, y_at(d)[1])
    order = (1, ny - 1, 2, ny - 2, 3, ny - 3, 4) if ny == 8 else (1,)
    for d in order:
        cy[d].wait_recv()
        pass_on(d)

    cut = (wx // 32) * 16
    if ny == 8:
        far[2].wait_recv()
        back = thr.at[0, y_at(ny - 2)[0]]
        far[3] = send((22, 22), back, back, y_at(1)[1])
        back = thr.at[0, y_at(ny - 2)[0], 0:cut]
        far["low"] = send((22, 22), back, back, y_at(2)[1])
        far[ny - 2].wait_recv()
        back = thr.at[0, y_at(2)[0]]
        far[ny - 3] = send((22, 22), back, back, y_at(ny - 1)[1])
        back = thr.at[0, y_at(2)[0], cut:wx]
        far["high"] = send((22, 22), back, back, y_at(ny - 2)[1])
    load("dec")
    arrive(c3)
    for k in range(nz):
        for j in range(ny):
            at = wx * (k * ny + j)
            gfull[0:4, at : at + wx] = gy[j, 4 * k : 4 * k + 4, 0:wx]

    arrive(c1)
    raw = pall[...].reshape(rows, tokens)
    row_t = lax.rem(lax.broadcasted_iota(jnp.int32, raw.shape, 0), 4)
    spot = lax.broadcasted_iota(jnp.int32, raw.shape, 1)
    row_pos = jnp.zeros(raw.shape, jnp.int32)
    own_pos = []
    for t in range(4):
        if t == 0:
            load("pos")
        own_pos.append(pos_ref[4 * g + t])
        row_pos = jnp.where(row_t == t, own_pos[t], row_pos)
    masked = jnp.where(spot <= row_pos, raw, 0.0)
    pattern = masked / jnp.sum(masked, axis=1, keepdims=True)
    pat = pattern.T
    pat_hi = pat.astype(bf16)
    pat_lo = (pat - pat_hi.astype(f32)).astype(bf16)
    pats[0] = pat_hi
    pats[1] = pat_lo

    straight = dot(gfull[...].astype(bf16), dec[...], NT)

    span = ny * wx
    sent.append((14, bx.at[0 : nx - 1]))
    late = [d for d in range(ny) if d not in early]
    for stage, ds in ((14, early), (15, late)):
        arrive((stage, bx.at[0 : nx - 1, 0 : len(ds)]))
        for d in ds:
            joined = [bx[i, d].astype(f32)[0:w] for i in range(nx)]
            thr[1, y_at(ny - d)[0]] = jnp.concatenate(joined, axis=0).astype(bf16)
    scores = dot(dec[:, span : 2 * span], thr[1].reshape(span, rows))
    sent.append((22, thr.at[0, 0 : ny - 1]))
    arrive((22, thr.at[0, 0 : ny - 3] if ny == 8 else thr.at[0, 0 : ny - 1]))
    if stop <= 9:
        return finish()
    scores += dot(dec[:, 0:span], thr[0].reshape(span, rows))
    sc_hi = scores.astype(bf16)
    sc_lo = (scores - sc_hi.astype(f32)).astype(bf16)
    right = jnp.concatenate([sc_hi, sc_hi, sc_lo], axis=1)

    ids = ids_t[...]
    act = act_ref[...]
    act = jnp.concatenate([act, act], axis=0)
    lane = lax.broadcasted_iota(jnp.int32, ids.shape, 1)
    pat_hi, pat_lo = pats[0], pats[1]
    of_t = lax.rem(lax.broadcasted_iota(jnp.int32, pat_hi.shape, 1), 4)
    token = lax.broadcasted_iota(jnp.int32, (tokens, feats), 0)
    piece = 2 * listed // ny
    summed, spread_out, placed = {}, {}, {}
    for p in range(2):
        picked = []
        for q in range(2):
            t = 2 * p + q
            hi = jnp.where(of_t == t, pat_hi, 0.0)
            lo = jnp.where(of_t == t, pat_lo, 0.0)
            left = jnp.concatenate([hi, lo, hi], axis=1)
            table = dot(left, right, NT)
            table += jnp.where(token == own_pos[t], straight[t : t + 1, :], 0.0)
            found = jnp.zeros(ids.shape, f32)
            for b in range(feats // 128):
                local = ids - 128 * b
                inside = (local >= 0) & (local < 128)
                taken = jnp.take_along_axis(
                    table[:, 128 * b : 128 * b + 128], jnp.clip(local, 0, 127), axis=1
                )
                found = jnp.where(inside, taken, found)
            picked.append(found)
        edge = jnp.where(lane < listed, picked[0], picked[1]).T * act
        edge = edge.astype(bf16)
        for j in range(ny):
            eparts[p, j] = edge[piece * j : piece * (j + 1)]
        summed[p] = exchange(
            10 if p == 0 else 19,
            "y",
            lambda who: eparts.at[p, who[1]],
            lambda d: ers.at[p, d],
            ers.at[p, 0 : ny - 1],
        )

    for p in range(2):
        arrive(summed[p])
        if stop <= 10 and p == 1:
            return finish()
        total = eparts[p, y]
        for d in range(1, ny):
            total += ers[p, d]
        eex[p, 0] = total
        spread_out[p] = exchange(
            11 if p == 0 else 20,
            "a",
            lambda who: eex.at[p, 0],
            lambda d: eex.at[p, d],
            eex.at[p, 0 : na - 1],
        )
    keep = {}
    for p in range(2):
        arrive(spread_out[p])
        total = eex[p, 0]
        for d in range(1, na):
            total += eex[p, d]
        e1[p] = total
        mine_out = out_ref.at[p, pl.ds(pl.multiple_of(y * piece, piece), piece), :]
        placed[p] = exchange(
            12 if p == 0 else 21,
            "y",
            lambda who: e1.at[p],
            lambda d: mine_out,
            ers.at[p, 0 : ny - 1],
        )
        keep[p] = pltpu.make_async_copy(e1.at[p], mine_out, in_sem.at[p])
        keep[p].start()
    for p in range(2):
        arrive(placed[p])
        keep[p].wait()
    finish()


def body(nz, ny, nx, nh, stop, cid, grads, positions, raw, out_proj, value_proj, decoders, ids, act):
    f32, bf16 = jnp.float32, jnp.bfloat16
    out_proj, value_proj, ids, act = out_proj.T, value_proj.T, ids.T, act.T
    w = grads.shape[1]
    listed, tokens = ids.shape
    feats, width = decoders.shape
    na, rows, piece = nz * nx, nh * 16, 2 * listed // ny
    wx = nx * w
    lanes_w = -(-w // 128) * 128
    lanes_x = -(-wx // 128) * 128
    tall_w = -(-w // 16) * 16
    vmem = pltpu.VMEM
    scratch = [
        pltpu.SMEM(positions.shape, jnp.int32),
        vmem(grads.shape, bf16),
        vmem(raw.shape, f32),
        vmem(out_proj.shape, bf16),
        vmem(value_proj.shape, bf16),
        vmem(ids.shape, jnp.int32),
        vmem(act.shape, f32),
        vmem((feats, width), bf16),
        vmem((nh, 8, lanes_w), f32),
        vmem((na, 8, lanes_w), f32),
        vmem((ny, 8, lanes_x), f32),
        vmem((8, width), f32),
        vmem((nh, 16, tokens), f32),
        vmem((nh, 16, tokens), f32),
        vmem((ny, 8, 2 * HD), f32),
        vmem((ny, 8, 2 * HD), f32),
        vmem((na, 8, 2 * HD), f32),
        vmem((ny, 8, 2 * HD), f32),
        vmem((nh, 16, lanes_w), bf16),
        vmem((nz, nh, 16, lanes_w), bf16),
        vmem((nx, tall_w, rows), bf16),
        vmem((nx, ny, tall_w, rows), bf16),
        vmem((nz, ny, wx, rows), bf16),
        vmem((2, ny, piece, tokens), bf16),
        vmem((2, ny, piece, tokens), bf16),
        vmem((2, piece, tokens), bf16),
        vmem((2, na, piece, tokens), bf16),
        vmem((2, tokens, rows), bf16),
        vmem((tokens, 2 * listed), jnp.int32),
        pltpu.SemaphoreType.DMA((8,)),
        pltpu.SemaphoreType.DMA((23,)),
        pltpu.SemaphoreType.DMA((32 + ny,)),
    ]
    in_hbm = [
        pltpu.with_memory_space_constraint(array, pltpu.HBM)
        for array in (positions, grads, raw, out_proj, value_proj, decoders, ids, act)
    ]
    edges = pl.pallas_call(
        functools.partial(kernel, nz, ny, nx, nh, stop),
        out_shape=jax.ShapeDtypeStruct((2, 2 * listed, tokens), bf16),
        in_specs=[pl.BlockSpec(memory_space=pltpu.HBM)] * 8,
        out_specs=pl.BlockSpec(memory_space=pltpu.VMEM),
        scratch_shapes=scratch,
        compiler_params=pltpu.CompilerParams(
            collective_id=cid, has_side_effects=True, vmem_limit_bytes=24 * 1024 * 1024
        ),
    )(*in_hbm)
    return edges.astype(f32).reshape(4, listed, tokens).transpose(0, 2, 1)


def solution(mesh, sizes=(NZ, NY, NX, NH), stop=99, cid=0):
    placed = (
        P("head", "feat"),
        P(),
        P("head", None, None),
        P("head", "feat"),
        P("head", "feat"),
        P("feat", None),
        P(),
        P(),
    )
    return jax.shard_map(
        functools.partial(body, *sizes, stop, cid),
        mesh=mesh,
        in_specs=placed,
        out_specs=P("head", None, None),
        check_vma=False,
    )
```

```python
import functools

import jax
import jax.numpy as jnp
from jax import lax
from jax.experimental import pallas as pl
from jax.experimental.pallas import tpu as pltpu
from jax.sharding import PartitionSpec as P

MESH = pl.DeviceIdType.MESH
HD = 128
NZ, NY, NX, NH = 2, 8, 4, 8
NT = (((1,), (1,)), ((), ()))


def dot(a, b, dims=(((1,), (0,)), ((), ()))):
    return lax.dot_general(a, b, dims, preferred_element_type=jnp.float32)


def kernel(
    nz, ny, nx, nh, stop,
    pos_hbm, grads_hbm, raw_hbm, outp_hbm, valp_hbm, dec_hbm, ids_hbm, act_hbm,
    out_ref,
    pos_ref, grads_ref, raw_ref, outp_ref, valp_ref, ids_ref, act_ref, dec, gall, ga, gy, gfull, pall, psend, part, rs, ex, hall, tsend, tall, ax, bx, thr,
    eparts, ers, e1, eex, pats, ids_t,
    in_sem, ssem, rsem,
):
    f32, bf16 = jnp.float32, jnp.bfloat16
    na = nz * nx
    w = grads_ref.shape[1]
    wx = nx * w
    listed, tokens = ids_ref.shape
    feats = dec.shape[0]
    rows = nh * 16
    f = lax.axis_index("feat")
    g = lax.axis_index("head")
    x = lax.rem(f, nx)
    y = lax.rem(lax.div(f, nx), ny)
    z = lax.div(f, nx * ny)
    a = z * nx + x

    def place(dz, dy, dx, dh):
        zj, yj, xj = lax.rem(z + dz, nz), lax.rem(y + dy, ny), lax.rem(x + dx, nx)
        gj = lax.rem(g + dh, nh)
        return zj, yj, xj, gj, (zj * (nx * ny) + yj * nx + xj, gj)

    def far_first(n):
        return sorted(range(1, n), key=lambda d: -min(d, n - d))

    groups = {
        "h": [(d, place(0, 0, 0, d)) for d in far_first(nh)],
        "y": [(d, place(0, d, 0, 0)) for d in far_first(ny)],
        "x": [(d, place(0, 0, d, 0)) for d in far_first(nx)],
        "a": [(nx * k + d, place(k, 0, d, 0)) for k in range(1, nz) for d in far_first(nx) + [0]]
        + [(d, place(0, 0, d, 0)) for d in far_first(nx)],
        "zh": [(d, place(1, 0, 0, d)) for d in [0] + far_first(nh)[::-1]],
    }

    barrier = pltpu.get_barrier_semaphore()
    greet = groups["a"] + groups["y"] + groups["zh"][1:] + groups["h"]
    greet = [who for slot, who in greet]
    for who in greet:
        pl.semaphore_signal(barrier, inc=1, device_id=who[4], device_id_type=MESH)

    loads = {}
    for i, (name, src, dst) in enumerate(
        (
            ("grads", grads_hbm, grads_ref),
            ("raw", raw_hbm, raw_ref),
            ("outp", outp_hbm, outp_ref),
            ("valp", valp_hbm, valp_ref),
            ("ids", ids_hbm, ids_ref),
            ("act", act_hbm, act_ref),
            ("pos", pos_hbm, pos_ref),
            ("dec", dec_hbm, dec),
        )
    ):
        loads[name] = pltpu.make_async_copy(src, dst, in_sem.at[i])
        loads[name].start()

    def load(name):
        loads[name].wait()
        loaded.append(name)

    def exchange(stage, group, src, dst, whole, each=None):
        copies = {}
        for slot, who in groups[group]:
            copies[slot] = pltpu.make_async_remote_copy(
                src_ref=src(who),
                dst_ref=dst(slot),
                send_sem=ssem.at[stage],
                recv_sem=rsem.at[stage if each is None else each + slot],
                device_id=who[4],
                device_id_type=MESH,
            )
            copies[slot].start()
        sent.append((stage, whole))
        return copies if each is not None else (stage, whole)

    def send(sems, src, dst, device):
        copy = pltpu.make_async_remote_copy(
            src_ref=src,
            dst_ref=dst,
            send_sem=ssem.at[sems[0]],
            recv_sem=rsem.at[sems[1]],
            device_id=device,
            device_id_type=MESH,
        )
        copy.start()
        return copy

    def all_of(stage, whole):
        return pltpu.make_async_remote_copy(
            src_ref=whole,
            dst_ref=whole,
            send_sem=ssem.at[stage],
            recv_sem=rsem.at[stage],
            device_id=groups["h"][0][1][4],
            device_id_type=MESH,
        )

    def arrive(one):
        all_of(*one).wait_recv()

    def finish():
        for one in sent:
            all_of(*one).wait_send()
        for name, copy in loads.items():
            if name not in loaded:
                copy.wait()

    sent, loaded = [], []

    load("grads")
    own = grads_ref[...].astype(f32)
    mine = jnp.concatenate([own, own], axis=0)
    zero_lanes = jnp.zeros((8, gall.shape[2]), f32)
    gall[g] = zero_lanes
    gall[g, :, 0:w] = mine
    ga[a] = zero_lanes
    ga[a, :, 0:w] = mine
    pl.semaphore_wait(barrier, len(greet))
    c0 = exchange(0, "h", lambda j: gall.at[g], lambda d: gall.at[g], gall.at[0 : nh - 1])

    load("raw")
    for j in range(nh):
        for h in range(4):
            psend[j, 4 * h : 4 * h + 4, :] = raw_ref[h, 4 * j : 4 * j + 4, :]
    tsend[...] = jnp.zeros_like(tsend)
    gfull[...] = jnp.zeros_like(gfull)
    load("outp")

    arrive(c0)
    if stop <= 0:
        return finish()
    both = gall[...].reshape(nh * 8, gall.shape[2])[:, 0:w]
    low = lax.rem(lax.broadcasted_iota(jnp.int32, both.shape, 0), 8) < 4
    half = 2 * HD
    partial = dot(jnp.where(low, both, 0.0).astype(bf16), outp_ref[:, 0:half])
    partial += dot(jnp.where(low, 0.0, both).astype(bf16), outp_ref[:, half : 2 * half])
    part[...] = partial.reshape(ny, 8, half)
    c4 = exchange(4, "y", lambda who: part.at[who[1]], lambda d: rs.at[d], rs.at[0 : ny - 1])
    c1 = exchange(1, "h", lambda who: psend.at[who[3]], lambda d: pall.at[g], pall.at[0 : nh - 1])
    pall[g] = psend[g]
    c2 = exchange(2, "a", lambda j: ga.at[a], lambda d: ga.at[a], ga.at[0 : na - 1])

    arrive(c4)
    if stop <= 4:
        return finish()
    total = part[y]
    for d in range(1, ny):
        total += rs[d]
    ex[0] = total
    c5 = exchange(5, "a", lambda j: ex.at[0], lambda d: ex.at[d], ex.at[0 : na - 1])

    arrive(c2)
    for k in range(nz):
        for i in range(nx):
            gy[y, 4 * k : 4 * k + 4, w * i : w * i + w] = ga[k * nx + i, 0:4, 0:w]
    c3 = exchange(3, "y", lambda j: gy.at[y], lambda d: gy.at[y], gy.at[0 : ny - 1])

    r = lax.broadcasted_iota(jnp.int32, (rows, ny * 8), 0)
    c = lax.broadcasted_iota(jnp.int32, (rows, ny * 8), 1)
    from_row = lax.div(r, 16) * 8 + lax.div(lax.rem(r, 16), 8) * 4 + lax.rem(r, 4)
    choose = (c == from_row).astype(bf16)
    r = lax.broadcasted_iota(jnp.int32, (rows, half), 0)
    lane = lax.broadcasted_iota(jnp.int32, (rows, half), 1)
    fits = lax.rem(lax.div(r, 4), 2) == lax.div(lane, HD)
    upper = lax.rem(lax.div(r, 8), 2) == 1

    arrive(c5)
    if stop <= 5:
        return finish()
    for d in range(1, na):
        total += ex[d]
    hall[y] = total.astype(bf16).astype(f32)
    c6 = exchange(6, "y", lambda j: hall.at[y], lambda d: hall.at[y], hall.at[0 : ny - 1])

    arrive(c6)
    if stop <= 6:
        return finish()
    hin = hall[...].reshape(ny * 8, half).astype(bf16)
    spread = dot(choose, hin)
    first = jnp.where(fits & ~upper, spread, 0.0).astype(bf16)
    second = jnp.where(fits & upper, spread, 0.0).astype(bf16)
    load("valp")
    through = dot(first, valp_ref[:, 0:half], NT)
    through += dot(second, valp_ref[:, half : 2 * half], NT)
    tsend[:, :, 0:w] = through.astype(bf16).reshape(nh, 16, w)
    c7 = exchange(7, "zh", lambda who: tsend.at[who[3]], lambda d: tall.at[z, g], tall.at[0])
    c13 = exchange(
        13, "h", lambda who: tsend.at[who[3]], lambda d: tall.at[z, g], tall.at[0, 0 : nh - 1]
    )
    tall[z, g] = tsend[g]

    load("ids")
    load("act")
    ids = ids_ref[...] - f * feats
    ids_t[...] = jnp.concatenate([ids, ids], axis=0).T

    arrive(c13)
    arrive(c7)
    if stop <= 7:
        return finish()
    low_w = ax.shape[2]
    tall_w = 2 * low_w

    def turned(k):
        block = tall[k].reshape(rows, tall.shape[3]).astype(f32).T
        return block[0:tall_w].astype(bf16)

    block = turned(0)
    ax[y, x] = block[0:low_w]
    cx = exchange(8, "x", lambda j: ax.at[y, x], lambda d: ax.at[y, x], ax.at[0, 0 : nx - 1])
    bx[x, 0, 0:tall_w] = turned(1)
    bx[x, 0, tall_w : tall_w + low_w] = block[low_w:tall_w]
    cy = exchange(9, "y", lambda j: bx.at[x, 0], lambda d: bx.at[x, d], bx.at[0, 0 : ny - 1], 24)
    def y_at(d):
        who = place(0, d, 0, 0)
        return who[1], who[4]

    hops = {}
    reach = ny // 2
    right, left = place(0, 0, 1, 0)[4], place(0, 0, nx - 1, 0)[4]
    from_left, from_right = lax.rem(x + nx - 1, nx), lax.rem(x + 1, nx)

    def pass_on(d):
        sems = (14, 32 + d if d < reach else 14)
        hops["r", d] = send(sems, bx.at[x, d], bx.at[x, d], right)
        sems = (15, 32 + d if d >= reach else 15)
        hops["l", d] = send(sems, bx.at[x, d], bx.at[x, d], left)

    def hand_on(d):
        if d < reach:
            hops["r", d].wait_recv()
            send((16, 16), bx.at[from_left, d], bx.at[from_left, d], right)
        else:
            hops["l", d].wait_recv()
            send((16, 17), bx.at[from_right, d], bx.at[from_right, d], left)

    pass_on(0)
    arrive(cx)
    mine_y = ax.at[y]
    far = {}
    steps = (2, ny - 2, 1, ny - 1) if ny == 8 else (1,)
    for i, d in enumerate(steps):
        far[d] = send((22, 23 + i if i < 2 and ny == 8 else 22), mine_y, mine_y, y_at(d)[1])
    order = (1, ny - 1, 2, ny - 2, 3, ny - 3, 4) if ny == 8 else (1,)
    for d in order:
        cy[d].wait_recv()
        pass_on(d)
    for d in ((0,) + order)[0:4]:
        hand_on(d)

    cut = nx // 2
    if ny == 8:
        far[2].wait_recv()
        back = ax.at[y_at(ny - 2)[0]]
        far[3] = send((22, 22), back, back, y_at(1)[1])
        back = ax.at[y_at(ny - 2)[0], 0:cut]
        far["low"] = send((22, 22), back, back, y_at(2)[1])
        far[ny - 2].wait_recv()
        back = ax.at[y_at(2)[0]]
        far[ny - 3] = send((22, 22), back, back, y_at(ny - 1)[1])
        back = ax.at[y_at(2)[0], cut:nx]
        far["high"] = send((22, 22), back, back, y_at(ny - 2)[1])
    for d in ((0,) + order)[4:]:
        hand_on(d)

    load("dec")
    arrive(c3)
    for k in range(nz):
        for j in range(ny):
            at = wx * (k * ny + j)
            gfull[0:4, at : at + wx] = gy[j, 4 * k : 4 * k + 4, 0:wx]

    arrive(c1)
    raw = pall[...].reshape(rows, tokens)
    row_t = lax.rem(lax.broadcasted_iota(jnp.int32, raw.shape, 0), 4)
    spot = lax.broadcasted_iota(jnp.int32, raw.shape, 1)
    row_pos = jnp.zeros(raw.shape, jnp.int32)
    own_pos = []
    for t in range(4):
        if t == 0:
            load("pos")
        own_pos.append(pos_ref[4 * g + t])
        row_pos = jnp.where(row_t == t, own_pos[t], row_pos)
    masked = jnp.where(spot <= row_pos, raw, 0.0)
    pattern = masked / jnp.sum(masked, axis=1, keepdims=True)
    pat = pattern.T
    pat_hi = pat.astype(bf16)
    pat_lo = (pat - pat_hi.astype(f32)).astype(bf16)
    pats[0] = pat_hi
    pats[1] = pat_lo

    straight = dot(gfull[...].astype(bf16), dec[...], NT)

    span = ny * wx
    sent.extend([(14, bx.at[0]), (15, bx.at[0]), (16, bx.at[0])])
    arrive((14, bx.at[0, 0 : ny - reach]))
    arrive((15, bx.at[0, 0:reach]))
    for stage, ds in ((16, range(reach)), (17, range(reach, ny))):
        arrive((stage, bx.at[0, 0 : len(ds)]))
        for d in ds:
            joined = [bx[i, d].astype(f32)[0:w] for i in range(nx)]
            thr[1, y_at(ny - d)[0]] = jnp.concatenate(joined, axis=0).astype(bf16)
    scores = dot(dec[:, span : 2 * span], thr[1].reshape(span, rows))
    sent.append((22, ax.at[0 : ny - 1]))
    arrive((22, ax.at[0 : ny - 3] if ny == 8 else ax.at[0 : ny - 1]))
    if stop <= 9:
        return finish()
    for d in range(ny):
        at = y_at(ny - d)[0]
        joined = []
        for i in range(nx):
            joined.append(ax[at, i].astype(f32))
            joined.append(bx[i, d, tall_w : tall_w + low_w].astype(f32)[0 : w - low_w])
        thr[0, at] = jnp.concatenate(joined, axis=0).astype(bf16)
    scores += dot(dec[:, 0:span], thr[0].reshape(span, rows))
    sc_hi = scores.astype(bf16)
    sc_lo = (scores - sc_hi.astype(f32)).astype(bf16)
    right = jnp.concatenate([sc_hi, sc_hi, sc_lo], axis=1)

    ids = ids_t[...]
    act = act_ref[...]
    act = jnp.concatenate([act, act], axis=0)
    lane = lax.broadcasted_iota(jnp.int32, ids.shape, 1)
    pat_hi, pat_lo = pats[0], pats[1]
    of_t = lax.rem(lax.broadcasted_iota(jnp.int32, pat_hi.shape, 1), 4)
    token = lax.broadcasted_iota(jnp.int32, (tokens, feats), 0)
    piece = 2 * listed // ny
    summed, spread_out, placed = {}, {}, {}
    for p in range(2):
        picked = []
        for q in range(2):
            t = 2 * p + q
            hi = jnp.where(of_t == t, pat_hi, 0.0)
            lo = jnp.where(of_t == t, pat_lo, 0.0)
            left = jnp.concatenate([hi, lo, hi], axis=1)
            table = dot(left, right, NT)
            table += jnp.where(token == own_pos[t], straight[t : t + 1, :], 0.0)
            found = jnp.zeros(ids.shape, f32)
            for b in range(feats // 128):
                local = ids - 128 * b
                inside = (local >= 0) & (local < 128)
                taken = jnp.take_along_axis(
                    table[:, 128 * b : 128 * b + 128], jnp.clip(local, 0, 127), axis=1
                )
                found = jnp.where(inside, taken, found)
            picked.append(found)
        edge = jnp.where(lane < listed, picked[0], picked[1]).T * act
        edge = edge.astype(bf16)
        for j in range(ny):
            eparts[p, j] = edge[piece * j : piece * (j + 1)]
        summed[p] = exchange(
            10 if p == 0 else 19,
            "y",
            lambda who: eparts.at[p, who[1]],
            lambda d: ers.at[p, d],
            ers.at[p, 0 : ny - 1],
        )

    for p in range(2):
        arrive(summed[p])
        if stop <= 10 and p == 1:
            return finish()
        total = eparts[p, y]
        for d in range(1, ny):
            total += ers[p, d]
        eex[p, 0] = total
        spread_out[p] = exchange(
            11 if p == 0 else 20,
            "a",
            lambda who: eex.at[p, 0],
            lambda d: eex.at[p, d],
            eex.at[p, 0 : na - 1],
        )
    keep = {}
    for p in range(2):
        arrive(spread_out[p])
        total = eex[p, 0]
        for d in range(1, na):
            total += eex[p, d]
        e1[p] = total
        mine_out = out_ref.at[p, pl.ds(pl.multiple_of(y * piece, piece), piece), :]
        placed[p] = exchange(
            12 if p == 0 else 21,
            "y",
            lambda who: e1.at[p],
            lambda d: mine_out,
            ers.at[p, 0 : ny - 1],
        )
        keep[p] = pltpu.make_async_copy(e1.at[p], mine_out, in_sem.at[p])
        keep[p].start()
    for p in range(2):
        arrive(placed[p])
        keep[p].wait()
    finish()


def body(nz, ny, nx, nh, stop, cid, grads, positions, raw, out_proj, value_proj, decoders, ids, act):
    f32, bf16 = jnp.float32, jnp.bfloat16
    out_proj, value_proj, ids, act = out_proj.T, value_proj.T, ids.T, act.T
    w = grads.shape[1]
    listed, tokens = ids.shape
    feats, width = decoders.shape
    na, rows, piece = nz * nx, nh * 16, 2 * listed // ny
    wx = nx * w
    lanes_w = -(-w // 128) * 128
    lanes_x = -(-wx // 128) * 128
    low_w = -(-w // 32) * 16
    vmem = pltpu.VMEM
    scratch = [
        pltpu.SMEM(positions.shape, jnp.int32),
        vmem(grads.shape, bf16),
        vmem(raw.shape, f32),
        vmem(out_proj.shape, bf16),
        vmem(value_proj.shape, bf16),
        vmem(ids.shape, jnp.int32),
        vmem(act.shape, f32),
        vmem((feats, width), bf16),
        vmem((nh, 8, lanes_w), f32),
        vmem((na, 8, lanes_w), f32),
        vmem((ny, 8, lanes_x), f32),
        vmem((8, width), f32),
        vmem((nh, 16, tokens), f32),
        vmem((nh, 16, tokens), f32),
        vmem((ny, 8, 2 * HD), f32),
        vmem((ny, 8, 2 * HD), f32),
        vmem((na, 8, 2 * HD), f32),
        vmem((ny, 8, 2 * HD), f32),
        vmem((nh, 16, lanes_w), bf16),
        vmem((nz, nh, 16, lanes_w), bf16),
        vmem((ny, nx, low_w, rows), bf16),
        vmem((nx, ny, 3 * low_w, rows), bf16),
        vmem((nz, ny, wx, rows), bf16),
        vmem((2, ny, piece, tokens), bf16),
        vmem((2, ny, piece, tokens), bf16),
        vmem((2, piece, tokens), bf16),
        vmem((2, na, piece, tokens), bf16),
        vmem((2, tokens, rows), bf16),
        vmem((tokens, 2 * listed), jnp.int32),
        pltpu.SemaphoreType.DMA((8,)),
        pltpu.SemaphoreType.DMA((23,)),
        pltpu.SemaphoreType.DMA((32 + ny,)),
    ]
    in_hbm = [
        pltpu.with_memory_space_constraint(array, pltpu.HBM)
        for array in (positions, grads, raw, out_proj, value_proj, decoders, ids, act)
    ]
    edges = pl.pallas_call(
        functools.partial(kernel, nz, ny, nx, nh, stop),
        out_shape=jax.ShapeDtypeStruct((2, 2 * listed, tokens), bf16),
        in_specs=[pl.BlockSpec(memory_space=pltpu.HBM)] * 8,
        out_specs=pl.BlockSpec(memory_space=pltpu.VMEM),
        scratch_shapes=scratch,
        compiler_params=pltpu.CompilerParams(
            collective_id=cid, has_side_effects=True, vmem_limit_bytes=24 * 1024 * 1024
        ),
    )(*in_hbm)
    return edges.astype(f32).reshape(4, listed, tokens).transpose(0, 2, 1)


def solution(mesh, sizes=(NZ, NY, NX, NH), stop=99, cid=0):
    placed = (
        P("head", "feat"),
        P(),
        P("head", None, None),
        P("head", "feat"),
        P("head", "feat"),
        P("feat", None),
        P(),
        P(),
    )
    return jax.shard_map(
        functools.partial(body, *sizes, stop, cid),
        mesh=mesh,
        in_specs=placed,
        out_specs=P("head", None, None),
        check_vma=False,
    )
```
